256 devices in a mesh: fsdp: 8 (over y, core), tile: 32 (over x, z).
Axes of the slice: x: 4, y: 4, z: 8, core: 2. Of those that a mesh axis runs over, the one named last changes fastest.
Arguments:
- tokens: bfloat16 [8, 4096, 1024], P('fsdp', 'tile'), may hold values from -8 to 8
- context: bfloat16 [8, 1024, 1024], P('fsdp', 'tile'), may hold values from -8 to 8
- pattern: int32 [8, 64, 16], P('fsdp', 'tile'), may hold values from 0 to 1, as said below
- w_query: bfloat16 [1024, 1024], P('fsdp'), may hold values from -0.125 to 0.125
- w_key: bfloat16 [1024, 1024], P('fsdp'), may hold values from -0.125 to 0.125
- w_value: bfloat16 [1024, 1024], P('fsdp'), may hold values from -0.1875 to 0.1875
- w_out: bfloat16 [1024, 1024], P('fsdp'), may hold values from -0.1875 to 0.1875
- cotangent: bfloat16 [8, 4096, 1024], P('fsdp', 'tile'), may hold values from -6 to 6
Outputs:
- mixed: bfloat16 [8, 4096, 1024], P('fsdp', 'tile')
- d_tokens: bfloat16 [8, 4096, 1024], P('fsdp', 'tile')
- d_context: bfloat16 [8, 1024, 1024], P('fsdp', 'tile')
- g_query: float32 [1024, 1024], P(('fsdp', 'tile'))
- g_out: float32 [1024, 1024], P(('fsdp', 'tile'))
The draws below stay inside these ranges and needn't reach their ends.
Inputs may be any that keep to these rules, and one draw needn't show every extreme that they name: `pattern`: every query block may attend at least one context block.
All inputs are finite; a program needn't handle non-finite values.
Results may differ from the reference program's by a relative error of at most 0.03.
The reference program's roundings to bfloat16 on the way (of `prob_low`, `attended`, `d_attended`, `d_score` and `d_queries`) count: a program that leaves them out, or rounds other values in their place, can miss the bound.
Values may be sent and summed in bfloat16 or wider, within the bound.
No kernel may reach another device: no remote copies, remote signals or barrier semaphores. Data moves between devices by JAX's collectives and lax.ppermute only.
A program may use at most 128 MiB of HBM per device.

```python
import math
import jax
import jax.numpy as jnp
from jax import lax

D = 1024
HEADS = 16
HEAD_DIM = 64
BLOCK = 64
TOK_DEV = 128
BATCH = 8
QLEN = 4096
KLEN = 1024
N_TILE = 32


def shared_matrix(key):
    base = jax.random.normal(key, (D, D), jnp.float32)
    return jnp.clip(base, -4.0, 4.0) / math.sqrt(D)


def draw_pattern(key, part):
    key = jax.random.fold_in(key, 7)
    key_level, key_coin, key_forced = jax.random.split(key, 3)
    q_blocks = QLEN // BLOCK
    k_blocks = KLEN // BLOCK
    level = jax.random.randint(key_level, (BATCH, q_blocks, 1), 1, 4)
    coins = jax.random.randint(key_coin, (BATCH, q_blocks, k_blocks), 0, 4)
    forced = jax.random.randint(key_forced, (BATCH, q_blocks, 1), 0, k_blocks)
    columns = jnp.arange(k_blocks)[None, None, :]
    return ((coins < level) | (columns == forced)).astype(jnp.int32)


def draw_w_query(key, part):
    return shared_matrix(key).astype(jnp.bfloat16)


def draw_w_key(key, part):
    key = jax.random.fold_in(key, 12)
    own = jnp.clip(jax.random.normal(key, (D, D), jnp.float32), -4.0, 4.0) / math.sqrt(D)
    return own.astype(jnp.bfloat16)


def draw_tokens(key, part):
    key = jax.random.fold_in(key, 13)
    key_noise = jax.random.fold_in(key, 0)
    noise = jnp.clip(jax.random.normal(key_noise, (BATCH, QLEN, D), jnp.float32), -6.0, 6.0)
    return noise.astype(jnp.bfloat16)


def draw_context(key, part):
    key = jax.random.fold_in(key, 14)
    key_noise = jax.random.fold_in(key, 0)
    noise = jnp.clip(jax.random.normal(key_noise, (BATCH, KLEN, D), jnp.float32), -6.0, 6.0)
    return noise.astype(jnp.bfloat16)


def levels(key, shape, pieces, smallest, high):
    factor_of = 1.0
    for dim, parts in pieces:
        heights = jax.random.uniform(jax.random.fold_in(jax.random.fold_in(key, 6), dim), (parts,), jnp.float32, smallest / len(pieces), high / len(pieces))
        factor_of = factor_of * jnp.repeat(jnp.exp(heights), shape[dim] // parts).reshape((-1,) + (1,) * (len(shape) - 1 - dim))
    return factor_of


def bell_draw(own_key, extent, scale, reach, cuts=(), dtype=jnp.bfloat16):
    entries = jax.random.normal(own_key, extent, jnp.float32) * scale
    if len(cuts) > 0:
        entries = levels(own_key, extent, cuts, -0.22, 0.18) * entries
    return jnp.clip(entries, min=-reach, max=reach).astype(dtype)


def setup_inputs(seed: int = 0) -> dict:
    arg_keys = jax.random.split(jax.random.key(seed), 9)
    tokens = draw_tokens(jax.random.fold_in(arg_keys[8], 71), 0)
    context = draw_context(jax.random.fold_in(arg_keys[8], 71), 0)
    pattern = draw_pattern(jax.random.fold_in(arg_keys[8], 71), 0)
    w_query = draw_w_query(jax.random.fold_in(arg_keys[8], 71), 0)
    w_key = draw_w_key(jax.random.fold_in(arg_keys[8], 71), 0)
    w_value = bell_draw(arg_keys[5], (D, D), D ** -0.5, 0.1875, ((0, 8),))
    w_out = bell_draw(arg_keys[6], (D, D), D ** -0.5, 0.1875, ((0, 8),))
    cotangent = bell_draw(arg_keys[7], (BATCH, QLEN, D), 1.0, 6.0, ((0, 8), (1, 32)))
    return {"tokens": tokens, "context": context, "pattern": pattern, "w_query": w_query, "w_key": w_key, "w_value": w_value, "w_out": w_out, "cotangent": cotangent}


def expand_mask(pattern_group):
    qb, kb = pattern_group.shape
    grid = pattern_group[:, None, :, None] > 0
    grid = jnp.broadcast_to(grid, (qb, BLOCK, kb, BLOCK))
    return grid.reshape(qb * BLOCK, kb * BLOCK)


def scene_pass(tok, ctx, pat, w_query, w_key, w_value, w_out, cot):
    f32 = jnp.float32
    bf16 = jnp.bfloat16
    queries = jnp.dot(tok, w_query, preferred_element_type=f32).astype(bf16)
    keys = jnp.dot(ctx, w_key, preferred_element_type=f32).astype(bf16)
    values = jnp.dot(ctx, w_value, preferred_element_type=f32).astype(bf16)
    d_attended = jnp.dot(cot, w_out.T, preferred_element_type=f32).astype(bf16)
    allowed = expand_mask(pat)

    def split_heads(mat):
        return jnp.transpose(mat.reshape(mat.shape[0], HEADS, HEAD_DIM), (1, 0, 2))

    def one_head(items):
        q_head, k_head, v_head, da_head = items
        scores = 0.125 * jnp.dot(q_head.astype(f32), k_head.astype(f32).T)
        scores = jnp.where(allowed, scores, -jnp.inf)
        top = jnp.max(scores, axis=1, keepdims=True)
        expo = jnp.exp(scores - top)
        attn_prob = expo / jnp.sum(expo, axis=1, keepdims=True)
        prob_low = attn_prob.astype(bf16)
        out_head = jnp.dot(prob_low, v_head, preferred_element_type=f32).astype(bf16)
        d_prob = jnp.dot(da_head.astype(f32), v_head.astype(f32).T)
        row_delta = jnp.sum(attn_prob * d_prob, axis=1, keepdims=True)
        d_score = (0.125 * attn_prob * (d_prob - row_delta)).astype(bf16)
        dq_head = jnp.dot(d_score, k_head, preferred_element_type=f32).astype(bf16)
        ds_runs = d_score.reshape(N_TILE, TOK_DEV, KLEN).astype(f32)
        pb_runs = prob_low.reshape(N_TILE, TOK_DEV, KLEN).astype(f32)
        q_runs = q_head.reshape(N_TILE, TOK_DEV, HEAD_DIM).astype(f32)
        da_runs = da_head.reshape(N_TILE, TOK_DEV, HEAD_DIM).astype(f32)
        dk_parts = jnp.einsum('tqk,tqd->tkd', ds_runs, q_runs).astype(bf16)
        dv_parts = jnp.einsum('tqk,tqd->tkd', pb_runs, da_runs).astype(bf16)
        dk_parts = lax.optimization_barrier(dk_parts).astype(f32)
        dv_parts = lax.optimization_barrier(dv_parts).astype(f32)
        return out_head, dq_head, jnp.sum(dk_parts, axis=0), jnp.sum(dv_parts, axis=0)

    outs = lax.map(one_head, (split_heads(queries), split_heads(keys), split_heads(values), split_heads(d_attended)))

    def join_heads(stack):
        return jnp.transpose(stack, (1, 0, 2)).reshape(stack.shape[1], D)

    attended = join_heads(outs[0])
    d_queries = join_heads(outs[1])
    d_keys = join_heads(outs[2])
    d_values = join_heads(outs[3])
    mixed = (tok.astype(f32) + jnp.dot(attended, w_out, preferred_element_type=f32)).astype(bf16)
    key_part = jnp.dot(d_keys, w_key.astype(f32).T, precision=lax.Precision.HIGHEST)
    value_part = jnp.dot(d_values, w_value.astype(f32).T, precision=lax.Precision.HIGHEST)
    d_context = (key_part + value_part).astype(bf16)
    d_tokens = (cot.astype(f32) + jnp.dot(d_queries, w_query.T, preferred_element_type=f32)).astype(bf16)
    g_query = jnp.dot(tok.T, d_queries, preferred_element_type=f32)
    g_out = jnp.dot(attended.T, cot, preferred_element_type=f32)
    return mixed, d_tokens, d_context, g_query, g_out


def reference(tokens, context, pattern, w_query, w_key, w_value, w_out, cotangent):
    mixed_list = []
    dtok_list = []
    dctx_list = []
    g_query = jnp.zeros((D, D), jnp.float32)
    g_out = jnp.zeros((D, D), jnp.float32)
    for scene in range(BATCH):
        result = scene_pass(tokens[scene], context[scene], pattern[scene], w_query, w_key, w_value, w_out, cotangent[scene])
        mixed_list.append(result[0])
        dtok_list.append(result[1])
        dctx_list.append(result[2])
        g_query = g_query + result[3]
        g_out = g_out + result[4]
    return jnp.stack(mixed_list), jnp.stack(dtok_list), jnp.stack(dctx_list), g_query, g_out
```

```python
import functools

import jax
import jax.numpy as jnp
from jax import lax
from jax.experimental import pallas as pl
from jax.experimental.pallas import tpu as pltpu
from jax.sharding import Mesh, PartitionSpec as P

BF = jnp.bfloat16
F32 = jnp.float32
X_SHIFTS = (0, 1, -1, 2)
Z_SHIFTS = (0, 4, 3, -3, 2, -2, 1, -1)
SIZES = {"y": 4, "c": 2, "x": 4, "z": 8}


def dot(a, b, da, db):
    return lax.dot_general(a, b, (((da,), (db,)), ((), ())), preferred_element_type=F32)


def shift(value, axis, by):
    n = SIZES[axis]
    return lax.ppermute(value, axis, [(i, (i + by) % n) for i in range(n)])


def mod(a, n):
    return lax.rem(a + n, n)


def kv_kernel(pos, c0, c1, c2, c3, wa, wb, kv_out, w_out, wo_out, ctx):
    y, c, x = pos[0], pos[1], pos[2]
    for src, by in zip((c0, c1, c2, c3), X_SHIFTS):
        at = pl.multiple_of(32 * mod(x - by, 4), 32)
        ctx[pl.ds(at, 32), :] = src[...]
    for half, core in ((wa, c), (wb, 1 - c)):
        for slot, by in enumerate(X_SHIFTS):
            at = pl.multiple_of(128 * (2 * mod(y - by, 4) + core), 128)
            w_out[pl.ds(at, 128), :] = half[128 * slot : 128 * slot + 128, 0:768]
        at = pl.multiple_of(128 * core, 128)
        for j in range(4):
            wo_out[pl.ds(at, 128), 256 * j : 256 * j + 256] = half[128 * j : 128 * j + 128, 768:1024]
    kv_out[...] = dot(ctx[...], w_out[:, 0:512], 1, 0).astype(BF)


def attn_kernel(pos, xg, kv0, kv1, kv2, kv3, kv4, kv5, kv6, kv7, w, wo, pay, att_out, dq_out,
                k_s, v_s, kt_s, vt_s, q_s, da_s, dk_s, dv_s, at_s, dqt_s, gq_s, go_s):
    z = pos[3]
    for src, by in zip((kv0, kv1, kv2, kv3, kv4, kv5, kv6, kv7), Z_SHIFTS):
        zs = mod(z - by, 8)
        for xs in range(4):
            at = pl.multiple_of(256 * xs + 32 * zs, 32)
            k_s[pl.ds(at, 32), :] = src[32 * xs : 32 * xs + 32, 0:256]
            v_s[pl.ds(at, 32), :] = src[32 * xs : 32 * xs + 32, 256:512]
    kt_s[...] = k_s[...].T
    vt_s[...] = v_s[...].T
    wq = w[:, 512:768]
    for t in range(4):
        rows = slice(128 * t, 128 * t + 128)
        q_s[rows, :] = dot(xg[t, 0:128, :], wq, 1, 0).astype(BF) * jnp.asarray(0.125, BF)
        da_s[rows, :] = dot(xg[t, 128:256, :], wo[...], 1, 1).astype(BF)
    dk_s[...] = jnp.zeros_like(dk_s)
    dv_s[...] = jnp.zeros_like(dv_s)
    lane = lax.broadcasted_iota(jnp.int32, (256, 128), 1) // 64
    row16 = lax.broadcasted_iota(jnp.int32, (16, 128), 0)
    col16 = lax.broadcasted_iota(jnp.int32, (16, 128), 1) // 64
    pick = jnp.where(row16 == col16, 1.0, 0.0).astype(BF)
    for u in range(2):
        allowed = jnp.concatenate(
            [dot(xg[2 * u + s, 256:272, :], pick, 0, 0) for s in range(2)], axis=1
        ) > 0.5
        for h in range(4):
            pair = slice(128 * (h // 2), 128 * (h // 2) + 128)
            head = slice(64 * h, 64 * h + 64)
            qrows = slice(256 * u, 256 * u + 256)
            own = lane == (h % 2)
            zero = jnp.zeros((256, 128), BF)
            qm = jnp.where(own, q_s[qrows, pair], zero)
            dam = jnp.where(own, da_s[qrows, pair], zero)
            s = jnp.where(allowed, dot(k_s[:, pair], qm, 1, 1), -jnp.inf)
            e = jnp.exp(s - jnp.max(s, axis=0, keepdims=True))
            p = e * (1.0 / jnp.sum(e, axis=0, keepdims=True))
            plow = p.astype(BF)
            at_s[head, qrows] = dot(vt_s[head, :], plow, 1, 0).astype(BF)
            dv_s[:, pair] += dot(plow, dam, 1, 0)
            dp = dot(v_s[:, pair], dam, 1, 1)
            delta = jnp.sum(p * dp, axis=0, keepdims=True)
            ds = (p * (dp - delta)).astype(BF)
            dqt_s[head, qrows] = (0.125 * dot(kt_s[head, :], ds, 1, 0)).astype(BF)
            dk_s[:, pair] += dot(ds, qm, 1, 0)
    att_out[...] = at_s[...].T
    dq_out[...] = dqt_s[...].T
    go = jnp.zeros((256, 1024), F32)
    gq = jnp.zeros((256, 1024), F32)
    for t in range(4):
        rows = slice(128 * t, 128 * t + 128)
        go += dot(at_s[:, rows], xg[t, 128:256, :], 1, 0)
        gq += dot(dqt_s[:, rows], xg[t, 0:128, :], 1, 0)
    for j in range(8):
        go_s[j] = go[:, 128 * j : 128 * j + 128]
    for j in range(2):
        gq_s[j] = gq[128 * j : 128 * j + 128, :].T
    for zd in range(8):
        base = 128 * zd
        for b in range(4):
            rows = slice(base + 32 * b, base + 32 * b + 32)
            keys = slice(256 * b + 32 * zd, 256 * b + 32 * zd + 32)
            pay[rows, 0:256] = dk_s[keys, :].astype(BF)
            pay[rows, 256:512] = dv_s[keys, :].astype(BF)
            for j in range(2):
                lanes = slice(512 + 128 * j, 640 + 128 * j)
                pay[rows, lanes] = gq_s[j, pl.ds(4 * zd + b, 32, stride=32), :].astype(BF)
                part = [go_s[2 * b + j, pl.ds(4 * zd + i, 8, stride=32), :] for i in range(4)]
                lanes = slice(768 + 128 * j, 896 + 128 * j)
                pay[rows, lanes] = jnp.concatenate(part, axis=0).astype(BF)


def md_kernel(att, dq, w, wo, out):
    for t in range(4):
        rows = slice(128 * t, 128 * t + 128)
        out[t, 0:128, :] = dot(att[rows, :], wo[...], 1, 0).astype(BF)
        out[t, 128:256, :] = dot(dq[rows, :], w[:, 512:768], 1, 1).astype(BF)


VM = pl.BlockSpec(memory_space=pltpu.VMEM)
SM = pl.BlockSpec(memory_space=pltpu.SMEM)


def call(kernel, n_in, outs, scratch, flops, nbytes, limit, name):
    return pl.pallas_call(
        kernel,
        out_shape=outs,
        in_specs=[SM] + [VM] * (n_in - 1) if name != "md" else [VM] * n_in,
        out_specs=[VM] * len(outs),
        scratch_shapes=scratch,
        compiler_params=pltpu.CompilerParams(vmem_limit_bytes=limit * 2**20),
        cost_estimate=pl.CostEstimate(flops=flops, bytes_accessed=nbytes, transcendentals=0),
        name=name,
    )


def local(tokens, context, pattern, w_query, w_key, w_value, w_out, cotangent):
    y, c, x, z = (lax.axis_index(n) for n in ("y", "c", "x", "z"))
    pos = jnp.stack([y, c, x, z]).astype(jnp.int32)
    tok, ctx, cot = tokens[0], context[0], cotangent[0]
    mask = jnp.repeat(pattern[0].astype(BF), 64, axis=1)
    own = jnp.concatenate([tok, cot, mask, jnp.zeros((14, 1024), BF)], axis=0)
    xg = lax.all_gather(own, "x", axis=0, tiled=False)

    ctxs = [ctx] + [shift(ctx, "x", by) for by in X_SHIFTS[1:]]
    col = 256 * x
    cut = lambda w: lax.dynamic_slice(w, (0, col), (128, 256))
    mine = jnp.concatenate([cut(w_key), cut(w_value), cut(w_query)], axis=1)
    slots = [mine] + [shift(mine, "y", by) for by in X_SHIFTS[1:]]
    wo = lax.ppermute(
        w_out, ("y", "x"), [(a * 4 + b, b * 4 + a) for a in range(4) for b in range(4)]
    )
    wo4 = jnp.concatenate([wo[:, 256 * j : 256 * j + 256] for j in range(4)], axis=0)
    wa = jnp.concatenate([jnp.concatenate(slots, axis=0), wo4], axis=1)
    wb = shift(wa, "c", 1)
    kv, w, wo_g = call(
        kv_kernel, 7,
        [jax.ShapeDtypeStruct((128, 512), BF), jax.ShapeDtypeStruct((1024, 768), BF),
         jax.ShapeDtypeStruct((256, 1024), BF)],
        [pltpu.VMEM((128, 1024), BF)], 2 * 128 * 1024 * 512, 4 * 2**20, 16, "kv",
    )(pos, *ctxs, wa, wb)

    kvs = [kv] + [shift(kv, "z", by) for by in Z_SHIFTS[1:]]
    pay, att, dq = call(
        attn_kernel, 12,
        [jax.ShapeDtypeStruct((1024, 1024), BF), jax.ShapeDtypeStruct((512, 256), BF),
         jax.ShapeDtypeStruct((512, 256), BF)],
        [pltpu.VMEM((1024, 256), BF), pltpu.VMEM((1024, 256), BF),
         pltpu.VMEM((256, 1024), BF), pltpu.VMEM((256, 1024), BF),
         pltpu.VMEM((512, 256), BF), pltpu.VMEM((512, 256), BF),
         pltpu.VMEM((1024, 256), F32), pltpu.VMEM((1024, 256), F32),
         pltpu.VMEM((256, 512), BF), pltpu.VMEM((256, 512), BF),
         pltpu.VMEM((2, 1024, 128), F32), pltpu.VMEM((8, 256, 128), F32)],
        2 * 1300 * 10**6, 8 * 2**20, 48, "attention",
    )(pos, xg, *kvs, w, wo_g)

    red = lax.psum_scatter(pay, "z", scatter_dimension=0, tiled=True)
    (md,) = call(
        md_kernel, 4, [jax.ShapeDtypeStruct((4, 256, 1024), BF)], [],
        2 * 2 * 512 * 256 * 1024, 4 * 2**20, 16, "md",
    )(att, dq, w, wo_g)
    md = lax.all_to_all(md, "x", split_axis=0, concat_axis=0, tiled=True)
    md = jnp.sum(md.astype(F32), axis=0)
    mixed = (tok.astype(F32) + md[0:128]).astype(BF)
    d_tokens = (cot.astype(F32) + md[128:256]).astype(BF)

    part = (dot(red[:, 0:256], w[:, 0:256], 1, 1) + dot(red[:, 256:512], w[:, 256:512], 1, 1)).astype(BF)
    part = lax.all_to_all(part.reshape(4, 32, 1024), "x", split_axis=0, concat_axis=0, tiled=True)
    d_context = jnp.sum(part.astype(F32), axis=0).astype(BF)

    gq = jnp.transpose(red[:, 512:768].reshape(4, 32, 256), (1, 0, 2))
    go = jnp.transpose(red[:, 768:1024].reshape(4, 4, 8, 256), (2, 1, 0, 3)).reshape(1, 8, 4, 1024)
    there = (jnp.arange(4) == x).reshape(4, 1, 1, 1)
    go = jnp.where(there, go, jnp.zeros((), BF)).reshape(32, 4, 1024)
    g = jnp.concatenate([gq, go], axis=2)
    g = lax.all_to_all(g, ("y", "c", "x"), split_axis=0, concat_axis=0, tiled=True).astype(F32)
    g_query = jnp.sum(g[:, :, 0:256].reshape(8, 4, 4, 256), axis=0)
    g_query = jnp.transpose(g_query, (1, 0, 2)).reshape(4, 1024)
    g_out = jnp.sum(g[:, :, 256:1280], axis=0)
    return mixed[None], d_tokens[None], d_context[None], g_query, g_out


def solution(mesh):
    fine = Mesh(mesh.devices.reshape(4, 2, 4, 8), ("y", "c", "x", "z"))
    seq = P(("y", "c"), ("x", "z"), None)
    wts = P(("y", "c"), None)
    grad = P(("y", "c", "x", "z"), None)
    return jax.shard_map(
        local,
        mesh=fine,
        in_specs=(seq, seq, seq, wts, wts, wts, wts, seq),
        out_specs=(seq, seq, seq, grad, grad),
        check_vma=False,
    )
```

```python
import jax
import jax.numpy as jnp
from jax import lax
from jax.experimental import pallas as pl
from jax.experimental.pallas import tpu as pltpu
from jax.sharding import Mesh, PartitionSpec as P

BF = jnp.bfloat16
F32 = jnp.float32
SHIFTS = (0, 1, -1, 2)
SIZES = {"y": 4, "c": 2, "x": 4, "z": 8}


def dot(a, b, da, db):
    return lax.dot_general(a, b, (((da,), (db,)), ((), ())), preferred_element_type=F32)


def shift(value, axis, by):
    n = SIZES[axis]
    return lax.ppermute(value, axis, [(i, (i + by) % n) for i in range(n)])


def mod(a, n):
    return lax.rem(a + n, n)


def pack_kernel(tok, cot, pattern, out):
    out[0:128, :] = tok[...]
    out[128:256, :] = cot[...]
    block = lax.broadcasted_iota(jnp.int32, (16, 1024), 0)
    key = lax.broadcasted_iota(jnp.int32, (16, 1024), 1)
    grow = jnp.where(block == 4 * ((key // 32) % 4) + key // 256, 1.0, 0.0).astype(BF)
    rows = jnp.where(pattern[...] == 1, 1.0, 0.0).astype(BF)
    rows = jnp.concatenate([rows, jnp.zeros((14, 16), BF)], axis=0)
    out[256:272, :] = dot(rows, grow, 1, 0).astype(BF)


def kv_kernel(pos, c0, c1, c2, c3, wa, wb, kv_out, w_out, ctx, sems):
    y, c, x = pos[0], pos[1], pos[2]
    copies = []
    for src, by in zip((c0, c1, c2, c3), SHIFTS):
        at = pl.multiple_of(32 * mod(x - by, 4), 32)
        copies.append((src, ctx.at[pl.ds(at, 32), :]))
    for half, core in ((wa, c), (wb, 1 - c)):
        for slot, by in enumerate(SHIFTS):
            at = pl.multiple_of(128 * (2 * mod(y - by, 4) + core), 128)
            copies.append((half.at[pl.ds(128 * slot, 128), :], w_out.at[pl.ds(at, 128), :]))
    copies = [pltpu.make_async_copy(a, b, sems.at[i]) for i, (a, b) in enumerate(copies)]
    for copy in copies:
        copy.start()
    for copy in copies:
        copy.wait()
    kv = dot(ctx[...], w_out[...], 1, 0).astype(BF)
    for zd in range(8):
        kv_out[zd] = kv


def qd_kernel(pos, xg, wa, wb, q_out, da_out, wq_out, wo_out, sems):
    y, c = pos[0], pos[1]
    copies = []
    for half, core in ((wa, c), (wb, 1 - c)):
        for slot, by in enumerate(SHIFTS):
            at = pl.multiple_of(128 * (2 * mod(y - by, 4) + core), 128)
            copies.append(
                (half.at[pl.ds(128 * slot, 128), 0:256], wq_out.at[pl.ds(at, 128), :])
            )
            at = pl.multiple_of(128 * core, 128)
            copies.append(
                (
                    half.at[pl.ds(128 * slot, 128), 256:512],
                    wo_out.at[pl.ds(at, 128), 256 * slot : 256 * slot + 256],
                )
            )
    copies = [pltpu.make_async_copy(a, b, sems.at[i]) for i, (a, b) in enumerate(copies)]
    for copy in copies:
        copy.start()
    for copy in copies:
        copy.wait()
    for t in range(4):
        rows = slice(128 * t, 128 * t + 128)
        q = dot(xg[t, 0:128, :], wq_out[...], 1, 0).astype(BF)
        q_out[rows, :] = q * jnp.asarray(0.125, BF)
        da_out[rows, :] = dot(xg[t, 128:256, :], wo_out[...], 1, 1).astype(BF)


def attn_kernel(xg, q_s, da_s, kv, pay, att_out, dq_out,
                kt_s, vt_s, dk_s, dv_s, at_s, dqt_s, gq_s, go_s, pay_s, mask_s, x_s, sems):
    mask_copies = [
        pltpu.make_async_copy(xg.at[t, pl.ds(256, 16), :], mask_s.at[t], sems.at[t])
        for t in range(4)
    ]
    x_copies = [
        pltpu.make_async_copy(xg.at[t, pl.ds(0, 256), :], x_s.at[t], sems.at[4 + t])
        for t in range(4)
    ]
    for copy in mask_copies + x_copies:
        copy.start()
    kt_s[...] = kv[:, 0:256].T
    vt_s[...] = kv[:, 256:512].T
    dk_s[...] = jnp.zeros_like(dk_s)
    dv_s[...] = jnp.zeros_like(dv_s)
    for copy in mask_copies:
        copy.wait()
    lane = lax.broadcasted_iota(jnp.int32, (256, 128), 1) // 64
    row16 = lax.broadcasted_iota(jnp.int32, (16, 128), 0)
    col16 = lax.broadcasted_iota(jnp.int32, (16, 128), 1) // 64
    pick = jnp.where(row16 == col16, 1.0, 0.0).astype(BF)
    for u in range(2):
        allowed = jnp.concatenate(
            [dot(mask_s[2 * u + s], pick, 0, 0) for s in range(2)], axis=1
        ) > 0.5
        for h in range(4):
            pair = slice(128 * (h // 2), 128 * (h // 2) + 128)
            vpair = slice(256 + 128 * (h // 2), 384 + 128 * (h // 2))
            head = slice(64 * h, 64 * h + 64)
            qrows = slice(256 * u, 256 * u + 256)
            own = lane == (h % 2)
            zero = jnp.zeros((256, 128), BF)
            qm = jnp.where(own, q_s[qrows, pair], zero)
            dam = jnp.where(own, da_s[qrows, pair], zero)
            s = jnp.where(allowed, dot(kv[:, pair], qm, 1, 1), -jnp.inf)
            e = jnp.exp(s - jnp.max(s, axis=0, keepdims=True))
            p = e * (1.0 / jnp.sum(e, axis=0, keepdims=True))
            plow = p.astype(BF)
            at_s[head, qrows] = dot(vt_s[head, :], plow, 1, 0).astype(BF)
            dv_s[:, pair] += dot(plow, dam, 1, 0)
            dp = dot(kv[:, vpair], dam, 1, 1)
            delta = jnp.sum(p * dp, axis=0, keepdims=True)
            ds = (p * (dp - delta)).astype(BF)
            dqt_s[head, qrows] = (0.125 * dot(kt_s[head, :], ds, 1, 0)).astype(BF)
            dk_s[:, pair] += dot(ds, qm, 1, 0)
    for copy in x_copies:
        copy.wait()
    go = jnp.zeros((256, 1024), F32)
    gq = jnp.zeros((256, 1024), F32)
    for t in range(4):
        rows = slice(128 * t, 128 * t + 128)
        go += dot(at_s[:, rows], x_s[t, 128:256, :], 1, 0)
        gq += dot(dqt_s[:, rows], x_s[t, 0:128, :], 1, 0)
    for j in range(8):
        go_s[j] = go[:, 128 * j : 128 * j + 128]
    for j in range(2):
        gq_s[j] = gq[128 * j : 128 * j + 128, :].T
    outs = []
    for zd in range(8):
        block = slice(128 * zd, 128 * zd + 128)
        pay_s[block, 0:256] = dk_s[block, :].astype(BF)
        pay_s[block, 256:512] = dv_s[block, :].astype(BF)
        for b in range(4):
            rows = slice(128 * zd + 32 * b, 128 * zd + 32 * b + 32)
            for j in range(2):
                lanes = slice(512 + 128 * j, 640 + 128 * j)
                pay_s[rows, lanes] = gq_s[j, pl.ds(4 * zd + b, 32, stride=32), :].astype(BF)
                part = [go_s[2 * b + j, pl.ds(4 * zd + i, 8, stride=32), :] for i in range(4)]
                lanes = slice(768 + 128 * j, 896 + 128 * j)
                pay_s[rows, lanes] = jnp.concatenate(part, axis=0).astype(BF)
        outs.append(pltpu.make_async_copy(pay_s.at[block, :], pay.at[block, :], sems.at[8 + zd]))
        outs[-1].start()
    att_out[...] = at_s[...].T
    dq_out[...] = dqt_s[...].T
    for copy in outs:
        copy.wait()


def md_kernel(att, dq, wq, wo, out):
    for t in range(4):
        rows = slice(128 * t, 128 * t + 128)
        out[t, 0:128, :] = dot(att[rows, :], wo[...], 1, 0).astype(BF)
        out[t, 128:256, :] = dot(dq[rows, :], wq[...], 1, 1).astype(BF)


def split_kernel(pos, red, w, p0, p1, p2, p3, g_out, part, g_s):
    x = pos[2]
    part[...] = dot(red[:, 0:256], w[:, 0:256], 1, 1) + dot(red[:, 256:512], w[:, 256:512], 1, 1)
    for out, by in zip((p0, p1, p2, p3), SHIFTS):
        at = pl.multiple_of(32 * mod(x + by, 4), 32)
        out[...] = part[pl.ds(at, 32), :].astype(BF)
    g_s[...] = jnp.zeros_like(g_s)
    for i in range(4):
        for j in range(2):
            lanes = slice(512 + 128 * j, 640 + 128 * j)
            rows = slice(32 * i, 32 * i + 32)
            g_s[pl.ds(2 * i + j, 32, stride=40), :] = red[rows, lanes].astype(F32)
    for b in range(4):
        for j in range(2):
            block = red[32 * b : 32 * b + 32, 768 + 128 * j : 896 + 128 * j].astype(F32)
            for i in range(4):
                at = 320 * x + 8 + 8 * i + 2 * b + j
                g_s[pl.ds(at, 8, stride=40), :] = block[8 * i : 8 * i + 8, :]
    g_out[...] = g_s[...].astype(BF)


def finish_kernel(g, p0, p1, p2, p3, dctx, g_query, g_out):
    total = p0[...].astype(F32)
    for p in (p1, p2, p3):
        total += p[...].astype(F32)
    dctx[...] = total.astype(BF)
    for xs in range(4):
        acc = jnp.zeros((8, 128), F32)
        for yc in range(8):
            at = 40 * (4 * yc + xs)
            acc += g[at : at + 8, :].astype(F32)
        for i in range(4):
            for j in range(2):
                row = 2 * i + j
                lanes = slice(256 * xs + 128 * j, 256 * xs + 128 * j + 128)
                g_query[i : i + 1, lanes] = acc[row : row + 1, :]
    acc = jnp.zeros((32, 128), F32)
    for src in range(32):
        acc += g[40 * src + 8 : 40 * src + 40, :].astype(F32)
    for i in range(4):
        for m in range(8):
            row = 8 * i + m
            g_out[i : i + 1, 128 * m : 128 * m + 128] = acc[row : row + 1, :]


V = pl.BlockSpec(memory_space=pltpu.VMEM)
S = pl.BlockSpec(memory_space=pltpu.SMEM)
A = pl.BlockSpec(memory_space=pl.ANY)


def sds(shape, dtype=BF):
    return jax.ShapeDtypeStruct(shape, dtype)


def call(kernel, in_specs, outs, scratch, mflop, kib, limit, name, out_specs=None):
    return pl.pallas_call(
        kernel,
        out_shape=outs,
        in_specs=in_specs,
        out_specs=out_specs or [V] * len(outs),
        scratch_shapes=scratch,
        compiler_params=pltpu.CompilerParams(vmem_limit_bytes=limit * 2**20),
        cost_estimate=pl.CostEstimate(
            flops=mflop * 10**6, bytes_accessed=kib * 1024, transcendentals=0
        ),
        name=name,
    )


def local(tokens, context, pattern, w_query, w_key, w_value, w_out, cotangent):
    y, c, x, z = (lax.axis_index(n) for n in ("y", "c", "x", "z"))
    pos = jnp.stack([y, c, x, z]).astype(jnp.int32)
    tok, ctx, cot = tokens[0], context[0], cotangent[0]
    (own,) = call(pack_kernel, [V, V, V], [sds((272, 1024))], [], 1, 1100, 8, "pack")(
        tok, cot, pattern[0]
    )
    xg = lax.all_gather(own, "x", axis=0, tiled=False)

    col = 256 * x
    cut = lambda w: lax.dynamic_slice(w, (0, col), (128, 256))
    mine = jnp.concatenate([cut(w_key), cut(w_value)], axis=1)
    wa = jnp.concatenate([mine] + [shift(mine, "y", by) for by in SHIFTS[1:]], axis=0)
    wb = shift(wa, "c", 1)
    ctxs = [ctx] + [shift(ctx, "x", by) for by in SHIFTS[1:]]
    kv8, wkv = call(
        kv_kernel, [S] + [A] * 6, [sds((8, 128, 512)), sds((1024, 512))],
        [pltpu.VMEM((128, 1024), BF), pltpu.SemaphoreType.DMA((12,))], 134, 3000, 16, "kv",
    )(pos, *ctxs, wa, wb)
    kvg = lax.all_to_all(kv8, "z", split_axis=0, concat_axis=0, tiled=True).reshape(1024, 512)

    w_query, w_out, kv8 = lax.optimization_barrier((w_query, w_out, kv8))
    mine = cut(w_query)
    wo = lax.ppermute(
        w_out, ("y", "x"), [(a * 4 + b, b * 4 + a) for a in range(4) for b in range(4)]
    )
    wo4 = jnp.concatenate([wo[:, 256 * j : 256 * j + 256] for j in range(4)], axis=0)
    wq4 = jnp.concatenate([mine] + [shift(mine, "y", by) for by in SHIFTS[1:]], axis=0)
    wa = jnp.concatenate([wq4, wo4], axis=1)
    wb = shift(wa, "c", 1)
    q, da, wq, wo = call(
        qd_kernel, [S, V, A, A],
        [sds((512, 256)), sds((512, 256)), sds((1024, 256)), sds((256, 1024))],
        [pltpu.SemaphoreType.DMA((16,))], 540, 5000, 24, "queries",
    )(pos, xg, wa, wb)

    pay, att, dq = call(
        attn_kernel, [A, V, V, V],
        [sds((1024, 1024)), sds((512, 256)), sds((512, 256))],
        [pltpu.VMEM((256, 1024), BF), pltpu.VMEM((256, 1024), BF),
         pltpu.VMEM((1024, 256), F32), pltpu.VMEM((1024, 256), F32),
         pltpu.VMEM((256, 512), BF), pltpu.VMEM((256, 512), BF),
         pltpu.VMEM((2, 1024, 128), F32), pltpu.VMEM((8, 256, 128), F32),
         pltpu.VMEM((1024, 1024), BF), pltpu.VMEM((4, 16, 1024), BF),
         pltpu.VMEM((4, 256, 1024), BF), pltpu.SemaphoreType.DMA((16,))],
        2200, 8000, 48, "attention", [A, V, V],
    )(xg, q, da, kvg)

    red = lax.psum_scatter(pay, "z", scatter_dimension=0, tiled=True)
    (md,) = call(md_kernel, [V] * 4, [sds((4, 256, 1024))], [], 540, 4000, 16, "md")(
        att, dq, wq, wo
    )
    md = lax.all_to_all(md, "x", split_axis=0, concat_axis=0, tiled=True)
    md = jnp.sum(md.astype(F32), axis=0)
    mixed = (tok.astype(F32) + md[0:128]).astype(BF)
    d_tokens = (cot.astype(F32) + md[128:256]).astype(BF)
    red, mixed, d_tokens = lax.optimization_barrier((red, mixed, d_tokens))

    *parts, g = call(
        split_kernel, [S, V, V], [sds((32, 1024))] * 4 + [sds((1280, 128))],
        [pltpu.VMEM((128, 1024), F32), pltpu.VMEM((1280, 128), F32)], 134, 2000, 16, "split",
    )(pos, red, wkv)
    parts = [parts[0]] + [shift(p, "x", by) for p, by in zip(parts[1:], SHIFTS[1:])]
    g = lax.all_to_all(
        g.reshape(32, 40, 128), ("y", "c", "x"), split_axis=0, concat_axis=0, tiled=True
    ).reshape(1280, 128)
    d_context, g_query, g_out = call(
        finish_kernel, [V] * 5, [sds((32, 1024)), sds((4, 1024), F32), sds((4, 1024), F32)],
        [], 1, 700, 8, "finish",
    )(g, *parts)
    return mixed[None], d_tokens[None], d_context[None], g_query, g_out


def solution(mesh):
    fine = Mesh(mesh.devices.reshape(4, 2, 4, 8), ("y", "c", "x", "z"))
    seq = P(("y", "c"), ("x", "z"), None)
    wts = P(("y", "c"), None)
    grad = P(("y", "c", "x", "z"), None)
    return jax.shard_map(
        local,
        mesh=fine,
        in_specs=(seq, seq, seq, wts, wts, wts, wts, seq),
        out_specs=(seq, seq, seq, grad, grad),
        check_vma=False,
    )
```

```python
import jax
import jax.numpy as jnp
from jax import lax
from jax.experimental import pallas as pl
from jax.experimental.pallas import tpu as pltpu
from jax.sharding import Mesh, PartitionSpec as P

BF = jnp.bfloat16
F32 = jnp.float32
SHIFTS = (0, 1, -1, 2)
SIZES = {"y": 4, "c": 2, "x": 4, "z": 8}


def dot(a, b, da, db):
    return lax.dot_general(a, b, (((da,), (db,)), ((), ())), preferred_element_type=F32)


def shift(value, axis, by):
    n = SIZES[axis]
    return lax.ppermute(value, axis, [(i, (i + by) % n) for i in range(n)])


def mod(a, n):
    return lax.rem(a + n, n)


def run_copies(pairs, sems):
    copies = [pltpu.make_async_copy(a, b, sems.at[i]) for i, (a, b) in enumerate(pairs)]
    for copy in copies:
        copy.start()
    return copies


def wait_all(copies):
    for copy in copies:
        copy.wait()


def pack_kernel(pos, tok, cot, pattern, wk, wv, wq, out, kv_cut, q_cut, pat_s, mask_s, sems):
    cols = pl.ds(pl.multiple_of(256 * pos[2], 256), 256)
    copies = run_copies(
        [
            (pattern, pat_s),
            (wk.at[:, cols], kv_cut.at[:, pl.ds(0, 256)]),
            (wv.at[:, cols], kv_cut.at[:, pl.ds(256, 256)]),
            (tok, out.at[pl.ds(0, 128), :]),
            (cot, out.at[pl.ds(128, 128), :]),
            (wq.at[:, cols], q_cut),
        ],
        sems,
    )
    block = lax.broadcasted_iota(jnp.int32, (16, 1024), 0)
    key = lax.broadcasted_iota(jnp.int32, (16, 1024), 1)
    grow = jnp.where(block == 4 * ((key // 32) % 4) + key // 256, 1.0, 0.0).astype(BF)
    copies[0].wait()
    rows = jnp.where(pat_s[...] == 1, 1.0, 0.0).astype(BF)
    rows = jnp.concatenate([rows, jnp.zeros((14, 16), BF)], axis=0)
    mask_s[...] = dot(rows, grow, 1, 0).astype(BF)
    last = pltpu.make_async_copy(mask_s, out.at[pl.ds(256, 16), :], sems.at[6])
    last.start()
    wait_all(copies[1:] + [last])


def kv_kernel(pos, c0, c1, c2, c3, wa, wb, kv_out, w_out, ctx, kv_s, sems):
    y, c, x = pos[0], pos[1], pos[2]
    pairs = []
    for half, core in ((wa, c), (wb, 1 - c)):
        for slot, by in enumerate(SHIFTS):
            at = pl.multiple_of(128 * (2 * mod(y - by, 4) + core), 128)
            pairs.append((half.at[pl.ds(128 * slot, 128), :], w_out.at[pl.ds(at, 128), :]))
    for src, by in zip((c0, c1, c2, c3), SHIFTS):
        at = pl.multiple_of(32 * mod(x - by, 4), 32)
        pairs.append((src, ctx.at[pl.ds(at, 32), :]))
    wait_all(run_copies(pairs, sems))
    kv_s[...] = dot(ctx[...], w_out[...], 1, 0).astype(BF)
    wait_all(run_copies([(kv_s, kv_out.at[zd]) for zd in range(8)], sems))


def qd_kernel(pos, xg, wa, wb, qd_out, wq_out, wo_out, x_s, wq_s, wo_s, q_s, da_s, sems):
    y, c = pos[0], pos[1]
    pairs = []
    for half, core in ((wa, c), (wb, 1 - c)):
        for slot, by in enumerate(SHIFTS):
            rows = pl.ds(128 * slot, 128)
            at = pl.multiple_of(128 * (2 * mod(y - by, 4) + core), 128)
            pairs.append((half.at[rows, pl.ds(0, 256)], wq_s.at[pl.ds(at, 128), :]))
            at = pl.multiple_of(128 * core, 128)
            lanes = pl.ds(256 * slot, 256)
            pairs.append((half.at[rows, pl.ds(256, 256)], wo_s.at[pl.ds(at, 128), lanes]))
    for t in range(4):
        for k in range(2):
            rows = pl.ds(128 * t, 128)
            pairs.append((xg.at[t, pl.ds(128 * k, 128), :], x_s.at[k, rows, :]))
    wait_all(run_copies(pairs, sems))
    q = dot(x_s[0], wq_s[...], 1, 0).astype(BF)
    q_s[...] = q * jnp.asarray(0.125, BF)
    da_s[...] = dot(x_s[1], wo_s[...], 1, 1).astype(BF)
    pairs = [(q_s, qd_out.at[0]), (da_s, qd_out.at[1]), (wq_s, wq_out), (wo_s, wo_out)]
    wait_all(run_copies(pairs, sems))


def attn_kernel(xg, qd, kv, pay, att_out, dq_out, q_s, da_s,
                kt_s, vt_s, dk_s, dv_s, at_s, dqt_s, gq_s, go_s, pay_s, mask_s, x_s, sems):
    mask_copies = [
        pltpu.make_async_copy(xg.at[t, pl.ds(256, 16), :], mask_s.at[t], sems.at[t])
        for t in range(4)
    ]
    x_copies = [
        pltpu.make_async_copy(
            xg.at[t, pl.ds(128 * k, 128), :], x_s.at[k, pl.ds(128 * t, 128), :], sems.at[4 + 4 * k + t]
        )
        for t in range(4)
        for k in range(2)
    ]
    mask_copies.append(pltpu.make_async_copy(qd.at[0], q_s, sems.at[20]))
    mask_copies.append(pltpu.make_async_copy(qd.at[1], da_s, sems.at[21]))
    for copy in mask_copies + x_copies:
        copy.start()
    kt_s[...] = kv[:, 0:256].T
    vt_s[...] = kv[:, 256:512].T
    dk_s[...] = jnp.zeros_like(dk_s)
    dv_s[...] = jnp.zeros_like(dv_s)
    for copy in mask_copies:
        copy.wait()
    lane = lax.broadcasted_iota(jnp.int32, (256, 128), 1) // 64
    row16 = lax.broadcasted_iota(jnp.int32, (16, 128), 0)
    col16 = lax.broadcasted_iota(jnp.int32, (16, 128), 1) // 64
    pick = jnp.where(row16 == col16, 1.0, 0.0).astype(BF)

    allowed = [
        jnp.concatenate([dot(mask_s[2 * u + s], pick, 0, 0) for s in range(2)], axis=1) > 0.5
        for u in range(2)
    ]
    zero = jnp.zeros((256, 128), BF)

    def first(u, h):
        pair = slice(128 * (h // 2), 128 * (h // 2) + 128)
        vpair = slice(256 + 128 * (h // 2), 384 + 128 * (h // 2))
        qrows = slice(256 * u, 256 * u + 256)
        own = lane == (h % 2)
        qm = jnp.where(own, q_s[qrows, pair], zero)
        dam = jnp.where(own, da_s[qrows, pair], zero)
        s = dot(kv[:, pair], qm, 1, 1)
        dp = dot(kv[:, vpair], dam, 1, 1)
        return qm, dam, s, dp

    def second(u, h, qm, dam, s, dp):
        pair = slice(128 * (h // 2), 128 * (h // 2) + 128)
        head = slice(64 * h, 64 * h + 64)
        qrows = slice(256 * u, 256 * u + 256)
        s = jnp.where(allowed[u], s, -jnp.inf)
        e = jnp.exp(s - jnp.max(s, axis=0, keepdims=True))
        p = e * (1.0 / jnp.sum(e, axis=0, keepdims=True))
        plow = p.astype(BF)
        delta = jnp.sum(p * dp, axis=0, keepdims=True)
        ds = (p * (dp - delta)).astype(BF)
        return plow, ds

    def third(u, h, qm, dam, plow, ds):
        pair = slice(128 * (h // 2), 128 * (h // 2) + 128)
        head = slice(64 * h, 64 * h + 64)
        qrows = slice(256 * u, 256 * u + 256)
        at_s[head, qrows] = dot(vt_s[head, :], plow, 1, 0).astype(BF)
        dqt_s[head, qrows] = (0.125 * dot(kt_s[head, :], ds, 1, 0)).astype(BF)
        dv_s[:, pair] += dot(plow, dam, 1, 0)
        dk_s[:, pair] += dot(ds, qm, 1, 0)


    units = [(u, h) for h in range(4) for u in range(2)]

    now = first(*units[0])
    for n, (u, h) in enumerate(units):
        later = first(*units[n + 1]) if n < 7 else None
        plow, ds = second(u, h, *now)
        third(u, h, now[0], now[1], plow, ds)
        now = later
    for copy in x_copies:
        copy.wait()
    go = dot(at_s[...], x_s[1], 1, 0)
    gq = dot(dqt_s[...], x_s[0], 1, 0)
    for j in range(8):
        go_s[j] = go[:, 128 * j : 128 * j + 128]
    for j in range(2):
        gq_s[j] = gq[128 * j : 128 * j + 128, :].T
    outs = []
    for zd in range(8):
        block = slice(128 * zd, 128 * zd + 128)
        pay_s[block, 0:256] = dk_s[block, :].astype(BF)
        pay_s[block, 256:512] = dv_s[block, :].astype(BF)
        for b in range(4):
            rows = slice(128 * zd + 32 * b, 128 * zd + 32 * b + 32)
            for j in range(2):
                lanes = slice(512 + 128 * j, 640 + 128 * j)
                pay_s[rows, lanes] = gq_s[j, pl.ds(4 * zd + b, 32, stride=32), :].astype(BF)
                part = [go_s[2 * b + j, pl.ds(4 * zd + i, 8, stride=32), :] for i in range(4)]
                lanes = slice(768 + 128 * j, 896 + 128 * j)
                pay_s[rows, lanes] = jnp.concatenate(part, axis=0).astype(BF)
        outs.append(pltpu.make_async_copy(pay_s.at[block, :], pay.at[block, :], sems.at[12 + zd]))
        outs[-1].start()
    att_out[...] = at_s[...].T
    dq_out[...] = dqt_s[...].T
    for copy in outs:
        copy.wait()


def md_kernel(att, dq, wq, wo, out):
    for t in range(4):
        rows = slice(128 * t, 128 * t + 128)
        out[t, 0:128, :] = dot(att[rows, :], wo[...], 1, 0).astype(BF)
        out[t, 128:256, :] = dot(dq[rows, :], wq[...], 1, 1).astype(BF)


def part_kernel(pos, red, w, p0, p1, p2, p3, part):
    x = pos[2]
    part[...] = dot(red[:, 0:256], w[:, 0:256], 1, 1) + dot(red[:, 256:512], w[:, 256:512], 1, 1)
    for out, by in zip((p0, p1, p2, p3), SHIFTS):
        at = pl.multiple_of(32 * mod(x + by, 4), 32)
        out[...] = part[pl.ds(at, 32), :].astype(BF)


def split_kernel(pos, red, g_out, g_s):
    x = pos[2]
    g_s[...] = jnp.zeros_like(g_s)
    for i in range(4):
        for j in range(2):
            lanes = slice(512 + 128 * j, 640 + 128 * j)
            rows = slice(32 * i, 32 * i + 32)
            g_s[pl.ds(2 * i + j, 32, stride=40), :] = red[rows, lanes].astype(F32)
    for b in range(4):
        for j in range(2):
            block = red[32 * b : 32 * b + 32, 768 + 128 * j : 896 + 128 * j].astype(F32)
            for i in range(4):
                at = 320 * x + 8 + 8 * i + 2 * b + j
                g_s[pl.ds(at, 8, stride=40), :] = block[8 * i : 8 * i + 8, :]
    g_out[...] = g_s[...].astype(BF)


def finish_kernel(g, p0, p1, p2, p3, dctx, g_query, g_out):
    total = p0[...].astype(F32)
    for p in (p1, p2, p3):
        total += p[...].astype(F32)
    dctx[...] = total.astype(BF)
    for xs in range(4):
        acc = jnp.zeros((8, 128), F32)
        for yc in range(8):
            at = 40 * (4 * yc + xs)
            acc += g[at : at + 8, :].astype(F32)
        for i in range(4):
            for j in range(2):
                row = 2 * i + j
                lanes = slice(256 * xs + 128 * j, 256 * xs + 128 * j + 128)
                g_query[i : i + 1, lanes] = acc[row : row + 1, :]
    acc = jnp.zeros((32, 128), F32)
    for src in range(32):
        acc += g[40 * src + 8 : 40 * src + 40, :].astype(F32)
    for i in range(4):
        for m in range(8):
            row = 8 * i + m
            g_out[i : i + 1, 128 * m : 128 * m + 128] = acc[row : row + 1, :]


V = pl.BlockSpec(memory_space=pltpu.VMEM)
S = pl.BlockSpec(memory_space=pltpu.SMEM)
H = pl.BlockSpec(memory_space=pltpu.HBM)


def sds(shape, dtype=BF):
    return jax.ShapeDtypeStruct(shape, dtype)


def call(kernel, in_specs, outs, scratch, mflop, kib, limit, name, out_specs=None):
    return pl.pallas_call(
        kernel,
        out_shape=outs,
        in_specs=in_specs,
        out_specs=out_specs or [V] * len(outs),
        scratch_shapes=scratch,
        compiler_params=pltpu.CompilerParams(vmem_limit_bytes=limit * 2**20),
        cost_estimate=pl.CostEstimate(
            flops=mflop * 10**6, bytes_accessed=kib * 1024, transcendentals=0
        ),
        name=name,
    )


def local(tokens, context, pattern, w_query, w_key, w_value, w_out, cotangent):
    y, c, x, z = (lax.axis_index(n) for n in ("y", "c", "x", "z"))
    pos = jnp.stack([y, c, x, z]).astype(jnp.int32)
    tok, ctx, cot = tokens[0], context[0], cotangent[0]
    own, mine, mine_q = call(
        pack_kernel, [S] + [H] * 6, [sds((272, 1024)), sds((128, 512)), sds((128, 256))],
        [pltpu.VMEM((2, 16), jnp.int32), pltpu.VMEM((16, 1024), BF), pltpu.SemaphoreType.DMA((7,))],
        1, 1500, 61, "pack", [H] * 3,
    )(pos, tok, cot, pattern[0], w_key, w_value, w_query)
    xg = lax.all_gather(own, "x", axis=0, tiled=False)

    ctxs = [ctx] + [shift(ctx, "x", by) for by in SHIFTS[1:]]
    wa = jnp.concatenate([mine] + [shift(mine, "y", by) for by in SHIFTS[1:]], axis=0)
    wa, *ctxs = lax.optimization_barrier((wa, *ctxs))
    wb = shift(wa, "c", 1)
    kv8, wkv = call(
        kv_kernel, [S] + [H] * 6, [sds((8, 128, 512)), sds((1024, 512))],
        [pltpu.VMEM((128, 1024), BF), pltpu.VMEM((128, 512), BF), pltpu.SemaphoreType.DMA((12,))],
        134, 3000, 16, "kv", [H, V],
    )(pos, *ctxs, wa, wb)
    kvg = lax.all_to_all(kv8, "z", split_axis=0, concat_axis=0, tiled=True).reshape(1024, 512)

    mine_q, w_out, kv8 = lax.optimization_barrier((mine_q, w_out, kv8))
    wo = lax.ppermute(
        w_out, ("y", "x"), [(a * 4 + b, b * 4 + a) for a in range(4) for b in range(4)]
    )
    wo4 = jnp.concatenate([wo[:, 256 * j : 256 * j + 256] for j in range(4)], axis=0)
    wq4 = jnp.concatenate([mine_q] + [shift(mine_q, "y", by) for by in SHIFTS[1:]], axis=0)
    wa = jnp.concatenate([wq4, wo4], axis=1)
    wb = shift(wa, "c", 1)
    qd, wq, wo = call(
        qd_kernel, [S, H, H, H],
        [sds((2, 512, 256)), sds((1024, 256)), sds((256, 1024))],
        [pltpu.VMEM((2, 512, 1024), BF), pltpu.VMEM((1024, 256), BF), pltpu.VMEM((256, 1024), BF),
         pltpu.VMEM((512, 256), BF), pltpu.VMEM((512, 256), BF), pltpu.SemaphoreType.DMA((24,))],
        540, 5000, 61, "queries", [H] * 3,
    )(pos, xg, wa, wb)

    pay, att, dq = call(
        attn_kernel, [H, H, V],
        [sds((1024, 1024)), sds((512, 256)), sds((512, 256))],
        [pltpu.VMEM((512, 256), BF), pltpu.VMEM((512, 256), BF),
         pltpu.VMEM((256, 1024), BF), pltpu.VMEM((256, 1024), BF),
         pltpu.VMEM((1024, 256), F32), pltpu.VMEM((1024, 256), F32),
         pltpu.VMEM((256, 512), BF), pltpu.VMEM((256, 512), BF),
         pltpu.VMEM((2, 1024, 128), F32), pltpu.VMEM((8, 256, 128), F32),
         pltpu.VMEM((1024, 1024), BF), pltpu.VMEM((4, 16, 1024), BF),
         pltpu.VMEM((2, 512, 1024), BF), pltpu.SemaphoreType.DMA((22,))],
        2200, 8000, 48, "attention", [H, V, V],
    )(xg, qd, kvg)

    red = lax.psum_scatter(pay, "z", scatter_dimension=0, tiled=True)
    (md,) = call(md_kernel, [V] * 4, [sds((4, 256, 1024))], [], 540, 4000, 16, "md")(
        att, dq, wq, wo
    )
    md = lax.all_to_all(md, "x", split_axis=0, concat_axis=0, tiled=True)
    md = jnp.sum(md.astype(F32), axis=0)
    mixed = (tok.astype(F32) + md[0:128]).astype(BF)
    d_tokens = (cot.astype(F32) + md[128:256]).astype(BF)
    red, mixed, d_tokens = lax.optimization_barrier((red, mixed, d_tokens))

    parts = call(
        part_kernel, [S, V, V], [sds((32, 1024))] * 4,
        [pltpu.VMEM((128, 1024), F32)], 134, 2000, 16, "part",
    )(pos, red, wkv)
    red, *parts = lax.optimization_barrier((red, *parts))
    (g,) = call(
        split_kernel, [S, V], [sds((1280, 128))], [pltpu.VMEM((1280, 128), F32)],
        1, 600, 16, "split",
    )(pos, red)
    parts = [parts[0]] + [shift(p, "x", by) for p, by in zip(parts[1:], SHIFTS[1:])]
    g = lax.all_to_all(
        g.reshape(32, 40, 128), ("y", "c", "x"), split_axis=0, concat_axis=0, tiled=True
    ).reshape(1280, 128)
    d_context, g_query, g_out = call(
        finish_kernel, [V] * 5, [sds((32, 1024)), sds((4, 1024), F32), sds((4, 1024), F32)],
        [], 1, 700, 8, "finish",
    )(g, *parts)
    return mixed[None], d_tokens[None], d_context[None], g_query, g_out


def solution(mesh):
    fine = Mesh(mesh.devices.reshape(4, 2, 4, 8), ("y", "c", "x", "z"))
    seq = P(("y", "c"), ("x", "z"), None)
    wts = P(("y", "c"), None)
    grad = P(("y", "c", "x", "z"), None)
    return jax.shard_map(
        local,
        mesh=fine,
        in_specs=(seq, seq, seq, wts, wts, wts, wts, seq),
        out_specs=(seq, seq, seq, grad, grad),
        check_vma=False,
    )
```

```python
import jax
import jax.numpy as jnp
from jax import lax
from jax.experimental import pallas as pl
from jax.experimental.pallas import tpu as pltpu
from jax.sharding import Mesh, PartitionSpec as P

BF = jnp.bfloat16
F32 = jnp.float32
SHIFTS = (0, 1, -1, 2)
SIZES = {"y": 4, "c": 2, "x": 4, "z": 8}


def dot(a, b, da, db):
    return lax.dot_general(a, b, (((da,), (db,)), ((), ())), preferred_element_type=F32)


def shift(value, axis, by):
    n = SIZES[axis]
    return lax.ppermute(value, axis, [(i, (i + by) % n) for i in range(n)])


def mod(a, n):
    return lax.rem(a + n, n)


def run_copies(pairs, sems):
    copies = [pltpu.make_async_copy(a, b, sems.at[i]) for i, (a, b) in enumerate(pairs)]
    for copy in copies:
        copy.start()
    return copies


def wait_all(copies):
    for copy in copies:
        copy.wait()


def pack_kernel(pos, tok, cot, pattern, wk, wv, wq, out, kv_cut, q_cut, pat_s, x_s, kv_s, q_s, sems):
    cols = pl.ds(pl.multiple_of(256 * pos[2], 256), 256)
    copies = run_copies(
        [
            (pattern, pat_s),
            (wk.at[:, cols], kv_s.at[:, pl.ds(0, 256)]),
            (wv.at[:, cols], kv_s.at[:, pl.ds(256, 256)]),
            (tok, x_s.at[pl.ds(0, 128), :]),
            (cot, x_s.at[pl.ds(128, 128), :]),
            (wq.at[:, cols], q_s),
        ],
        sems,
    )
    block = lax.broadcasted_iota(jnp.int32, (16, 1024), 0)
    key = lax.broadcasted_iota(jnp.int32, (16, 1024), 1)
    grow = jnp.where(block == 4 * ((key // 32) % 4) + key // 256, 1.0, 0.0).astype(BF)
    copies[0].wait()
    rows = jnp.where(pat_s[...] == 1, 1.0, 0.0).astype(BF)
    rows = jnp.concatenate([rows, jnp.zeros((14, 16), BF)], axis=0)
    x_s[256:272, :] = dot(rows, grow, 1, 0).astype(BF)
    wait_all(copies[1:])
    wait_all(run_copies([(x_s, out), (kv_s, kv_cut), (q_s, q_cut)], sems))


def kv_kernel(pos, c0, c1, c2, c3, wa, wb, kv_out, w_out, ctx, w_s, kv_s, sems):
    y, c, x = pos[0], pos[1], pos[2]
    for half, core in ((wa, c), (wb, 1 - c)):
        for slot, by in enumerate(SHIFTS):
            at = pl.multiple_of(128 * (2 * mod(y - by, 4) + core), 128)
            w_s[pl.ds(at, 128), :] = half[128 * slot : 128 * slot + 128, :]
    for src, by in zip((c0, c1, c2, c3), SHIFTS):
        at = pl.multiple_of(32 * mod(x - by, 4), 32)
        ctx[pl.ds(at, 32), :] = src[...]
    kv_s[...] = dot(ctx[...], w_s[...], 1, 0).astype(BF)
    pairs = [(kv_s, kv_out.at[zd]) for zd in range(8)] + [(w_s, w_out)]
    wait_all(run_copies(pairs, sems))


def qd_kernel(pos, xg, wa, wb, qd_out, wq_out, wo_out, x_s, wq_s, wo_s, q_s, da_s, sems):
    y, c = pos[0], pos[1]
    pairs = []
    for half, core in ((wa, c), (wb, 1 - c)):
        for slot, by in enumerate(SHIFTS):
            rows = pl.ds(128 * slot, 128)
            at = pl.multiple_of(128 * (2 * mod(y - by, 4) + core), 128)
            pairs.append((half.at[rows, pl.ds(0, 256)], wq_s.at[pl.ds(at, 128), :]))
            at = pl.multiple_of(128 * core, 128)
            lanes = pl.ds(256 * slot, 256)
            pairs.append((half.at[rows, pl.ds(256, 256)], wo_s.at[pl.ds(at, 128), lanes]))
    for t in range(4):
        for k in range(2):
            rows = pl.ds(128 * t, 128)
            pairs.append((xg.at[t, pl.ds(128 * k, 128), :], x_s.at[k, rows, :]))
    wait_all(run_copies(pairs, sems))
    q = dot(x_s[0], wq_s[...], 1, 0).astype(BF)
    q_s[...] = q * jnp.asarray(0.125, BF)
    da_s[...] = dot(x_s[1], wo_s[...], 1, 1).astype(BF)
    pairs = [(q_s, qd_out.at[0]), (da_s, qd_out.at[1]), (wq_s, wq_out), (wo_s, wo_out)]
    wait_all(run_copies(pairs, sems))


def attn_kernel(xg, qd, kv, pay, att_out, dq_out, q_s, da_s,
                kt_s, vt_s, dk_s, dv_s, at_s, dqt_s, gq_s, go_s, pay_s, mask_s, x_s, sems):
    mask_copies = [
        pltpu.make_async_copy(xg.at[t, pl.ds(256, 16), :], mask_s.at[t], sems.at[t])
        for t in range(4)
    ]
    x_copies = [
        pltpu.make_async_copy(
            xg.at[t, pl.ds(128 * k, 128), :], x_s.at[k, pl.ds(128 * t, 128), :], sems.at[4 + 4 * k + t]
        )
        for t in range(4)
        for k in range(2)
    ]
    mask_copies.append(pltpu.make_async_copy(qd.at[0], q_s, sems.at[20]))
    mask_copies.append(pltpu.make_async_copy(qd.at[1], da_s, sems.at[21]))
    for copy in mask_copies + x_copies:
        copy.start()
    kt_s[...] = kv[:, 0:256].T
    vt_s[...] = kv[:, 256:512].T
    dk_s[...] = jnp.zeros_like(dk_s)
    dv_s[...] = jnp.zeros_like(dv_s)
    for copy in mask_copies:
        copy.wait()
    lane = lax.broadcasted_iota(jnp.int32, (256, 128), 1) // 64
    row16 = lax.broadcasted_iota(jnp.int32, (16, 128), 0)
    col16 = lax.broadcasted_iota(jnp.int32, (16, 128), 1) // 64
    pick = jnp.where(row16 == col16, 1.0, 0.0).astype(BF)

    allowed = [
        jnp.concatenate([dot(mask_s[2 * u + s], pick, 0, 0) for s in range(2)], axis=1) > 0.5
        for u in range(2)
    ]
    zero = jnp.zeros((256, 128), BF)

    def first(u, h):
        pair = slice(128 * (h // 2), 128 * (h // 2) + 128)
        vpair = slice(256 + 128 * (h // 2), 384 + 128 * (h // 2))
        qrows = slice(256 * u, 256 * u + 256)
        own = lane == (h % 2)
        qm = jnp.where(own, q_s[qrows, pair], zero)
        dam = jnp.where(own, da_s[qrows, pair], zero)
        s = dot(kv[:, pair], qm, 1, 1)
        dp = dot(kv[:, vpair], dam, 1, 1)
        return qm, dam, s, dp

    def second(u, h, qm, dam, s, dp):
        pair = slice(128 * (h // 2), 128 * (h // 2) + 128)
        head = slice(64 * h, 64 * h + 64)
        qrows = slice(256 * u, 256 * u + 256)
        s = jnp.where(allowed[u], s, -jnp.inf)
        e = jnp.exp(s - jnp.max(s, axis=0, keepdims=True))
        p = e * (1.0 / jnp.sum(e, axis=0, keepdims=True))
        plow = p.astype(BF)
        delta = jnp.sum(p * dp, axis=0, keepdims=True)
        ds = (p * (dp - delta)).astype(BF)
        return plow, ds

    def third(u, h, qm, dam, plow, ds):
        pair = slice(128 * (h // 2), 128 * (h // 2) + 128)
        head = slice(64 * h, 64 * h + 64)
        qrows = slice(256 * u, 256 * u + 256)
        at_s[head, qrows] = dot(vt_s[head, :], plow, 1, 0).astype(BF)
        dqt_s[head, qrows] = (0.125 * dot(kt_s[head, :], ds, 1, 0)).astype(BF)
        dv_s[:, pair] += dot(plow, dam, 1, 0)
        dk_s[:, pair] += dot(ds, qm, 1, 0)


    units = [(u, h) for h in range(4) for u in range(2)]

    now = first(*units[0])
    for n, (u, h) in enumerate(units):
        later = first(*units[n + 1]) if n < 7 else None
        plow, ds = second(u, h, *now)
        third(u, h, now[0], now[1], plow, ds)
        now = later
    for copy in x_copies:
        copy.wait()
    go = dot(at_s[...], x_s[1], 1, 0)
    gq = dot(dqt_s[...], x_s[0], 1, 0)
    for j in range(8):
        go_s[j] = go[:, 128 * j : 128 * j + 128]
    for j in range(2):
        gq_s[j] = gq[128 * j : 128 * j + 128, :].T
    outs = []
    for zd in range(8):
        block = slice(128 * zd, 128 * zd + 128)
        pay_s[block, 0:256] = dk_s[block, :].astype(BF)
        pay_s[block, 256:512] = dv_s[block, :].astype(BF)
        for b in range(4):
            rows = slice(128 * zd + 32 * b, 128 * zd + 32 * b + 32)
            for j in range(2):
                lanes = slice(512 + 128 * j, 640 + 128 * j)
                pay_s[rows, lanes] = gq_s[j, pl.ds(4 * zd + b, 32, stride=32), :].astype(BF)
                part = [go_s[2 * b + j, pl.ds(4 * zd + i, 8, stride=32), :] for i in range(4)]
                lanes = slice(768 + 128 * j, 896 + 128 * j)
                pay_s[rows, lanes] = jnp.concatenate(part, axis=0).astype(BF)
        outs.append(pltpu.make_async_copy(pay_s.at[block, :], pay.at[block, :], sems.at[12 + zd]))
        outs[-1].start()
    att_out[...] = at_s[...].T
    dq_out[...] = dqt_s[...].T
    for copy in outs:
        copy.wait()


def md_kernel(att, dq, wq, wo, out):
    for t in range(4):
        rows = slice(128 * t, 128 * t + 128)
        out[t, 0:128, :] = dot(att[rows, :], wo[...], 1, 0).astype(BF)
        out[t, 128:256, :] = dot(dq[rows, :], wq[...], 1, 1).astype(BF)


def part_kernel(pos, red, w, p0, p1, p2, p3, part):
    x = pos[2]
    part[...] = dot(red[:, 0:256], w[:, 0:256], 1, 1) + dot(red[:, 256:512], w[:, 256:512], 1, 1)
    for out, by in zip((p0, p1, p2, p3), SHIFTS):
        at = pl.multiple_of(32 * mod(x + by, 4), 32)
        out[...] = part[pl.ds(at, 32), :].astype(BF)


def split_kernel(pos, red, g_out, g_s):
    x = pos[2]
    g_s[...] = jnp.zeros_like(g_s)
    for i in range(4):
        for j in range(2):
            lanes = slice(512 + 128 * j, 640 + 128 * j)
            rows = slice(32 * i, 32 * i + 32)
            g_s[pl.ds(2 * i + j, 32, stride=40), :] = red[rows, lanes].astype(F32)
    for b in range(4):
        for j in range(2):
            block = red[32 * b : 32 * b + 32, 768 + 128 * j : 896 + 128 * j].astype(F32)
            for i in range(4):
                at = 320 * x + 8 + 8 * i + 2 * b + j
                g_s[pl.ds(at, 8, stride=40), :] = block[8 * i : 8 * i + 8, :]
    g_out[...] = g_s[...].astype(BF)


def finish_kernel(g, p0, p1, p2, p3, dctx, g_query, g_out):
    total = p0[...].astype(F32)
    for p in (p1, p2, p3):
        total += p[...].astype(F32)
    dctx[...] = total.astype(BF)
    for xs in range(4):
        acc = jnp.zeros((8, 128), F32)
        for yc in range(8):
            at = 40 * (4 * yc + xs)
            acc += g[at : at + 8, :].astype(F32)
        for i in range(4):
            for j in range(2):
                row = 2 * i + j
                lanes = slice(256 * xs + 128 * j, 256 * xs + 128 * j + 128)
                g_query[i : i + 1, lanes] = acc[row : row + 1, :]
    acc = jnp.zeros((32, 128), F32)
    for src in range(32):
        acc += g[40 * src + 8 : 40 * src + 40, :].astype(F32)
    for i in range(4):
        for m in range(8):
            row = 8 * i + m
            g_out[i : i + 1, 128 * m : 128 * m + 128] = acc[row : row + 1, :]


V = pl.BlockSpec(memory_space=pltpu.VMEM)
S = pl.BlockSpec(memory_space=pltpu.SMEM)
H = pl.BlockSpec(memory_space=pltpu.HBM)


def sds(shape, dtype=BF):
    return jax.ShapeDtypeStruct(shape, dtype)


def call(kernel, in_specs, outs, scratch, mflop, kib, limit, name, out_specs=None):
    return pl.pallas_call(
        kernel,
        out_shape=outs,
        in_specs=in_specs,
        out_specs=out_specs or [V] * len(outs),
        scratch_shapes=scratch,
        compiler_params=pltpu.CompilerParams(vmem_limit_bytes=limit * 2**20),
        cost_estimate=pl.CostEstimate(
            flops=mflop * 10**6, bytes_accessed=kib * 1024, transcendentals=0
        ),
        name=name,
    )


def local(tokens, context, pattern, w_query, w_key, w_value, w_out, cotangent):
    y, c, x, z = (lax.axis_index(n) for n in ("y", "c", "x", "z"))
    pos = jnp.stack([y, c, x, z]).astype(jnp.int32)
    tok, ctx, cot = tokens[0], context[0], cotangent[0]
    own, mine, mine_q = call(
        pack_kernel, [S] + [H] * 6, [sds((272, 1024)), sds((128, 512)), sds((128, 256))],
        [pltpu.VMEM((2, 16), jnp.int32), pltpu.VMEM((272, 1024), BF), pltpu.VMEM((128, 512), BF),
         pltpu.VMEM((128, 256), BF), pltpu.SemaphoreType.DMA((6,))],
        1, 1500, 61, "pack", [H] * 3,
    )(pos, tok, cot, pattern[0], w_key, w_value, w_query)
    xg = lax.all_gather(own, "x", axis=0, tiled=False)

    ctxs = [ctx] + [shift(ctx, "x", by) for by in SHIFTS[1:]]
    wa = jnp.concatenate([mine] + [shift(mine, "y", by) for by in SHIFTS[1:]], axis=0)
    wa, *ctxs = lax.optimization_barrier((wa, *ctxs))
    wb = shift(wa, "c", 1)
    kv8, wkv = call(
        kv_kernel, [S] + [V] * 6, [sds((8, 128, 512)), sds((1024, 512))],
        [pltpu.VMEM((128, 1024), BF), pltpu.VMEM((1024, 512), BF), pltpu.VMEM((128, 512), BF),
         pltpu.SemaphoreType.DMA((9,))],
        134, 3000, 16, "kv", [H, H],
    )(pos, *ctxs, wa, wb)
    kvg = lax.all_to_all(kv8, "z", split_axis=0, concat_axis=0, tiled=True).reshape(1024, 512)

    mine_q, w_out, kv8 = lax.optimization_barrier((mine_q, w_out, kv8))
    wo = lax.ppermute(
        w_out, ("y", "x"), [(a * 4 + b, b * 4 + a) for a in range(4) for b in range(4)]
    )
    wo4 = jnp.concatenate([wo[:, 256 * j : 256 * j + 256] for j in range(4)], axis=0)
    wq4 = jnp.concatenate([mine_q] + [shift(mine_q, "y", by) for by in SHIFTS[1:]], axis=0)
    wa = jnp.concatenate([wq4, wo4], axis=1)
    wb = shift(wa, "c", 1)
    qd, wq, wo = call(
        qd_kernel, [S, H, H, H],
        [sds((2, 512, 256)), sds((1024, 256)), sds((256, 1024))],
        [pltpu.VMEM((2, 512, 1024), BF), pltpu.VMEM((1024, 256), BF), pltpu.VMEM((256, 1024), BF),
         pltpu.VMEM((512, 256), BF), pltpu.VMEM((512, 256), BF), pltpu.SemaphoreType.DMA((24,))],
        540, 5000, 61, "queries", [H] * 3,
    )(pos, xg, wa, wb)

    pay, att, dq = call(
        attn_kernel, [H, H, V],
        [sds((1024, 1024)), sds((512, 256)), sds((512, 256))],
        [pltpu.VMEM((512, 256), BF), pltpu.VMEM((512, 256), BF),
         pltpu.VMEM((256, 1024), BF), pltpu.VMEM((256, 1024), BF),
         pltpu.VMEM((1024, 256), F32), pltpu.VMEM((1024, 256), F32),
         pltpu.VMEM((256, 512), BF), pltpu.VMEM((256, 512), BF),
         pltpu.VMEM((2, 1024, 128), F32), pltpu.VMEM((8, 256, 128), F32),
         pltpu.VMEM((1024, 1024), BF), pltpu.VMEM((4, 16, 1024), BF),
         pltpu.VMEM((2, 512, 1024), BF), pltpu.SemaphoreType.DMA((22,))],
        2200, 8000, 48, "attention", [H, V, V],
    )(xg, qd, kvg)

    red = lax.psum_scatter(pay, "z", scatter_dimension=0, tiled=True)
    (md,) = call(md_kernel, [V] * 4, [sds((4, 256, 1024))], [], 540, 4000, 16, "md")(
        att, dq, wq, wo
    )
    md = lax.all_to_all(md, "x", split_axis=0, concat_axis=0, tiled=True)
    md = jnp.sum(md.astype(F32), axis=0)
    mixed = (tok.astype(F32) + md[0:128]).astype(BF)
    d_tokens = (cot.astype(F32) + md[128:256]).astype(BF)
    red, mixed, d_tokens = lax.optimization_barrier((red, mixed, d_tokens))

    parts = call(
        part_kernel, [S, V, V], [sds((32, 1024))] * 4,
        [pltpu.VMEM((128, 1024), F32)], 134, 2000, 16, "part",
    )(pos, red, wkv)
    red, *parts = lax.optimization_barrier((red, *parts))
    (g,) = call(
        split_kernel, [S, V], [sds((1280, 128))], [pltpu.VMEM((1280, 128), F32)],
        1, 600, 16, "split",
    )(pos, red)
    parts = [parts[0]] + [shift(p, "x", by) for p, by in zip(parts[1:], SHIFTS[1:])]
    g = lax.all_to_all(
        g.reshape(32, 40, 128), ("y", "c", "x"), split_axis=0, concat_axis=0, tiled=True
    ).reshape(1280, 128)
    d_context, g_query, g_out = call(
        finish_kernel, [V] * 5, [sds((32, 1024)), sds((4, 1024), F32), sds((4, 1024), F32)],
        [], 1, 700, 8, "finish",
    )(g, *parts)
    return mixed[None], d_tokens[None], d_context[None], g_query, g_out


def solution(mesh):
    fine = Mesh(mesh.devices.reshape(4, 2, 4, 8), ("y", "c", "x", "z"))
    seq = P(("y", "c"), ("x", "z"), None)
    wts = P(("y", "c"), None)
    grad = P(("y", "c", "x", "z"), None)
    return jax.shard_map(
        local,
        mesh=fine,
        in_specs=(seq, seq, seq, wts, wts, wts, wts, seq),
        out_specs=(seq, seq, seq, grad, grad),
        check_vma=False,
    )
```

```python
import jax
import jax.numpy as jnp
from jax import lax
from jax.experimental import pallas as pl
from jax.experimental.pallas import tpu as pltpu
from jax.sharding import Mesh, PartitionSpec as P

BF = jnp.bfloat16
F32 = jnp.float32
SHIFTS = (0, 1, -1, 2)
SIZES = {"y": 4, "c": 2, "x": 4, "z": 8}


def dot(a, b, da, db):
    return lax.dot_general(a, b, (((da,), (db,)), ((), ())), preferred_element_type=F32)


def shift(value, axis, by):
    n = SIZES[axis]
    return lax.ppermute(value, axis, [(i, (i + by) % n) for i in range(n)])


def mod(a, n):
    return lax.rem(a + n, n)


def run_copies(pairs, sems):
    copies = [pltpu.make_async_copy(a, b, sems.at[i]) for i, (a, b) in enumerate(pairs)]
    for copy in copies:
        copy.start()
    return copies


def wait_all(copies):
    for copy in copies:
        copy.wait()


def pack_kernel(pos, tok, cot, pattern, wk, wv, wq, out, kv_cut, q_cut, pat_s, x_s, kv_s, q_s, sems):
    cols = pl.ds(pl.multiple_of(256 * pos[2], 256), 256)
    copies = run_copies(
        [
            (pattern, pat_s),
            (wk.at[:, cols], kv_s.at[:, pl.ds(0, 256)]),
            (wv.at[:, cols], kv_s.at[:, pl.ds(256, 256)]),
            (tok, x_s.at[pl.ds(0, 128), :]),
            (cot, x_s.at[pl.ds(128, 128), :]),
            (wq.at[:, cols], q_s),
        ],
        sems,
    )
    block = lax.broadcasted_iota(jnp.int32, (16, 1024), 0)
    key = lax.broadcasted_iota(jnp.int32, (16, 1024), 1)
    grow = jnp.where(block == 4 * ((key // 32) % 4) + key // 256, 1.0, 0.0).astype(BF)
    copies[0].wait()
    rows = jnp.where(pat_s[...] == 1, 1.0, 0.0).astype(BF)
    rows = jnp.concatenate([rows, jnp.zeros((14, 16), BF)], axis=0)
    x_s[256:272, :] = dot(rows, grow, 1, 0).astype(BF)
    wait_all(copies[1:])
    wait_all(run_copies([(x_s, out), (kv_s, kv_cut), (q_s, q_cut)], sems))


def kv_kernel(pos, c0, c1, c2, c3, wa, wb, kv_out, w_out, ctx, w_s, kv_s, sems):
    y, c, x = pos[0], pos[1], pos[2]
    for half, core in ((wa, c), (wb, 1 - c)):
        for slot, by in enumerate(SHIFTS):
            at = pl.multiple_of(128 * (2 * mod(y - by, 4) + core), 128)
            w_s[pl.ds(at, 128), :] = half[128 * slot : 128 * slot + 128, :]
    for src, by in zip((c0, c1, c2, c3), SHIFTS):
        at = pl.multiple_of(32 * mod(x - by, 4), 32)
        ctx[pl.ds(at, 32), :] = src[...]
    kv_s[...] = dot(ctx[...], w_s[...], 1, 0).astype(BF)
    pairs = [(kv_s, kv_out.at[zd]) for zd in range(8)] + [(w_s, w_out)]
    wait_all(run_copies(pairs, sems))


def qd_kernel(pos, xg, wa, wb, qd_out, wq_out, wo_out, x_s, wq_s, wo_s, q_s, da_s, sems):
    y, c = pos[0], pos[1]
    pairs = []
    for half, core in ((wa, c), (wb, 1 - c)):
        for slot, by in enumerate(SHIFTS):
            rows = pl.ds(128 * slot, 128)
            at = pl.multiple_of(128 * (2 * mod(y - by, 4) + core), 128)
            pairs.append((half.at[rows, pl.ds(0, 256)], wq_s.at[pl.ds(at, 128), :]))
            at = pl.multiple_of(128 * core, 128)
            lanes = pl.ds(256 * slot, 256)
            pairs.append((half.at[rows, pl.ds(256, 256)], wo_s.at[pl.ds(at, 128), lanes]))
    for t in range(4):
        for k in range(2):
            rows = pl.ds(128 * t, 128)
            pairs.append((xg.at[t, pl.ds(128 * k, 128), :], x_s.at[k, rows, :]))
    wait_all(run_copies(pairs, sems))
    q = dot(x_s[0], wq_s[...], 1, 0).astype(BF)
    q_s[...] = q * jnp.asarray(0.125, BF)
    da_s[...] = dot(x_s[1], wo_s[...], 1, 1).astype(BF)
    pairs = [(q_s, qd_out.at[0]), (da_s, qd_out.at[1]), (wq_s, wq_out), (wo_s, wo_out)]
    wait_all(run_copies(pairs, sems))


def attn_kernel(xg, qd, kv, pay, att_out, dq_out, at_s, dqt_s, q_s, da_s,
                kt_s, vt_s, dk_s, dv_s, pay_s, mask_s, sems):
    mask_copies = [
        pltpu.make_async_copy(xg.at[t, pl.ds(256, 16), :], mask_s.at[t], sems.at[t])
        for t in range(4)
    ]
    mask_copies.append(pltpu.make_async_copy(qd.at[0], q_s, sems.at[4]))
    mask_copies.append(pltpu.make_async_copy(qd.at[1], da_s, sems.at[5]))
    for copy in mask_copies:
        copy.start()
    kt_s[...] = kv[:, 0:256].T
    vt_s[...] = kv[:, 256:512].T
    dk_s[...] = jnp.zeros_like(dk_s)
    dv_s[...] = jnp.zeros_like(dv_s)
    for copy in mask_copies:
        copy.wait()
    lane = lax.broadcasted_iota(jnp.int32, (256, 128), 1) // 64
    row16 = lax.broadcasted_iota(jnp.int32, (16, 128), 0)
    col16 = lax.broadcasted_iota(jnp.int32, (16, 128), 1) // 64
    pick = jnp.where(row16 == col16, 1.0, 0.0).astype(BF)

    allowed = [
        jnp.concatenate([dot(mask_s[2 * u + s], pick, 0, 0) for s in range(2)], axis=1) > 0.5
        for u in range(2)
    ]
    zero = jnp.zeros((256, 128), BF)

    def first(u, h):
        pair = slice(128 * (h // 2), 128 * (h // 2) + 128)
        vpair = slice(256 + 128 * (h // 2), 384 + 128 * (h // 2))
        qrows = slice(256 * u, 256 * u + 256)
        own = lane == (h % 2)
        qm = jnp.where(own, q_s[qrows, pair], zero)
        dam = jnp.where(own, da_s[qrows, pair], zero)
        s = dot(kv[:, pair], qm, 1, 1)
        dp = dot(kv[:, vpair], dam, 1, 1)
        return qm, dam, s, dp

    def second(u, h, qm, dam, s, dp):
        pair = slice(128 * (h // 2), 128 * (h // 2) + 128)
        head = slice(64 * h, 64 * h + 64)
        qrows = slice(256 * u, 256 * u + 256)
        s = jnp.where(allowed[u], s, -jnp.inf)
        e = jnp.exp(s - jnp.max(s, axis=0, keepdims=True))
        p = e * (1.0 / jnp.sum(e, axis=0, keepdims=True))
        plow = p.astype(BF)
        delta = jnp.sum(p * dp, axis=0, keepdims=True)
        ds = (p * (dp - delta)).astype(BF)
        return plow, ds

    def third(u, h, qm, dam, plow, ds):
        pair = slice(128 * (h // 2), 128 * (h // 2) + 128)
        head = slice(64 * h, 64 * h + 64)
        qrows = slice(256 * u, 256 * u + 256)
        at_s[head, qrows] = dot(vt_s[head, :], plow, 1, 0).astype(BF)
        dqt_s[head, qrows] = (0.125 * dot(kt_s[head, :], ds, 1, 0)).astype(BF)
        dv_s[:, pair] += dot(plow, dam, 1, 0)
        dk_s[:, pair] += dot(ds, qm, 1, 0)


    units = [(u, h) for h in range(4) for u in range(2)]

    now = first(*units[0])
    for n, (u, h) in enumerate(units):
        later = first(*units[n + 1]) if n < 7 else None
        plow, ds = second(u, h, *now)
        third(u, h, now[0], now[1], plow, ds)
        now = later
    outs = []
    for zd in range(8):
        block = slice(128 * zd, 128 * zd + 128)
        pay_s[block, 0:256] = dk_s[block, :].astype(BF)
        pay_s[block, 256:512] = dv_s[block, :].astype(BF)
        outs.append(pltpu.make_async_copy(pay_s.at[block, :], pay.at[block, :], sems.at[6 + zd]))
        outs[-1].start()
    att_out[...] = at_s[...].T
    dq_out[...] = dqt_s[...].T
    wait_all(outs)


def g_kernel(xg, at, dqt, out, x_s, o_s, sems):
    pairs = []
    for t in range(4):
        for k in range(2):
            rows = pl.ds(128 * t, 128)
            pairs.append((xg.at[t, pl.ds(128 * k, 128), :], x_s.at[k, rows, :]))
    wait_all(run_copies(pairs, sems))
    go = dot(at[...], x_s[1], 1, 0)
    gq = dot(dqt[...], x_s[0], 1, 0).T
    for d in range(8):
        o_s[d, :, 0:256] = gq[128 * d : 128 * d + 128, :].astype(BF)
        base = 32 * (4 * (d % 2) + d // 2)
        for b in range(4):
            part = go[base : base + 32, 256 * b : 256 * b + 256]
            o_s[d, 32 * b : 32 * b + 32, 256:512] = part.astype(BF)
    wait_all(run_copies([(o_s, out)], sems))


def gsum_kernel(g, gq_out, go_out):
    total = g[0].astype(F32)
    for d in range(1, 8):
        total += g[d].astype(F32)
    gq_out[...] = total[:, 0:256].astype(BF)
    for b in range(4):
        go_out[:, 256 * b : 256 * b + 256] = total[32 * b : 32 * b + 32, 256:512].astype(BF)


def md_kernel(pos, att, dq, wq, wo, m0, m1, m2, m3):
    for out, by in zip((m0, m1, m2, m3), SHIFTS):
        rows = pl.ds(pl.multiple_of(128 * mod(pos[2] + by, 4), 128), 128)
        out[0:128, :] = dot(att[rows, :], wo[...], 1, 0).astype(BF)
        out[128:256, :] = dot(dq[rows, :], wq[...], 1, 1).astype(BF)


def part_kernel(pos, red, w, p0, p1, p2, p3, part):
    x = pos[2]
    part[...] = dot(red[:, 0:256], w[:, 0:256], 1, 1) + dot(red[:, 256:512], w[:, 256:512], 1, 1)
    for out, by in zip((p0, p1, p2, p3), SHIFTS):
        at = pl.multiple_of(32 * mod(x + by, 4), 32)
        out[...] = part[pl.ds(at, 32), :].astype(BF)


def split_kernel(pos, gq, go, g_out, g_s, gq_s, go_s):
    x = pos[2]
    g_s[...] = jnp.zeros_like(g_s)
    for j in range(2):
        gq_s[j] = gq[:, 128 * j : 128 * j + 128].astype(F32)
    for m in range(8):
        go_s[m] = go[:, 128 * m : 128 * m + 128].astype(F32)
    for i in range(4):
        for j in range(2):
            g_s[pl.ds(2 * i + j, 32, stride=40), :] = gq_s[j, pl.ds(i, 32, stride=4), :]
        for m in range(8):
            at = 320 * x + 8 + 8 * i + m
            g_s[pl.ds(at, 8, stride=40), :] = go_s[m, pl.ds(i, 8, stride=4), :]
    g_out[...] = g_s[...].astype(BF)


def finish_kernel(g, p0, p1, p2, p3, dctx, g_query, g_out):
    total = p0[...].astype(F32)
    for p in (p1, p2, p3):
        total += p[...].astype(F32)
    dctx[...] = total.astype(BF)
    for xs in range(4):
        acc = jnp.zeros((8, 128), F32)
        for zs in range(8):
            at = 40 * (8 * xs + zs)
            acc += g[at : at + 8, :].astype(F32)
        for i in range(4):
            for j in range(2):
                row = 2 * i + j
                lanes = slice(256 * xs + 128 * j, 256 * xs + 128 * j + 128)
                g_query[i : i + 1, lanes] = acc[row : row + 1, :]
    acc = jnp.zeros((32, 128), F32)
    for src in range(32):
        acc += g[40 * src + 8 : 40 * src + 40, :].astype(F32)
    for i in range(4):
        for m in range(8):
            row = 8 * i + m
            g_out[i : i + 1, 128 * m : 128 * m + 128] = acc[row : row + 1, :]


V = pl.BlockSpec(memory_space=pltpu.VMEM)
S = pl.BlockSpec(memory_space=pltpu.SMEM)
H = pl.BlockSpec(memory_space=pltpu.HBM)


def sds(shape, dtype=BF):
    return jax.ShapeDtypeStruct(shape, dtype)


def call(kernel, in_specs, outs, scratch, mflop, kib, limit, name, out_specs=None):
    return pl.pallas_call(
        kernel,
        out_shape=outs,
        in_specs=in_specs,
        out_specs=out_specs or [V] * len(outs),
        scratch_shapes=scratch,
        compiler_params=pltpu.CompilerParams(vmem_limit_bytes=limit * 2**20),
        cost_estimate=pl.CostEstimate(
            flops=mflop * 10**6, bytes_accessed=kib * 1024, transcendentals=0
        ),
        name=name,
    )


def local(tokens, context, pattern, w_query, w_key, w_value, w_out, cotangent):
    y, c, x, z = (lax.axis_index(n) for n in ("y", "c", "x", "z"))
    pos = jnp.stack([y, c, x, z]).astype(jnp.int32)
    tok, ctx, cot = tokens[0], context[0], cotangent[0]
    own, mine, mine_q = call(
        pack_kernel, [S] + [H] * 6, [sds((272, 1024)), sds((128, 512)), sds((128, 256))],
        [pltpu.VMEM((2, 16), jnp.int32), pltpu.VMEM((272, 1024), BF), pltpu.VMEM((128, 512), BF),
         pltpu.VMEM((128, 256), BF), pltpu.SemaphoreType.DMA((6,))],
        1, 1500, 61, "pack", [H] * 3,
    )(pos, tok, cot, pattern[0], w_key, w_value, w_query)
    xg = lax.all_gather(own, "x", axis=0, tiled=False)

    ctxs = [ctx] + [shift(ctx, "x", by) for by in SHIFTS[1:]]
    wa = jnp.concatenate([mine] + [shift(mine, "y", by) for by in SHIFTS[1:]], axis=0)
    wa, *ctxs = lax.optimization_barrier((wa, *ctxs))
    wb = shift(wa, "c", 1)
    kv8, wkv = call(
        kv_kernel, [S] + [V] * 6, [sds((8, 128, 512)), sds((1024, 512))],
        [pltpu.VMEM((128, 1024), BF), pltpu.VMEM((1024, 512), BF), pltpu.VMEM((128, 512), BF),
         pltpu.SemaphoreType.DMA((9,))],
        134, 3000, 16, "kv", [H, H],
    )(pos, *ctxs, wa, wb)
    kvg = lax.all_to_all(kv8, "z", split_axis=0, concat_axis=0, tiled=True).reshape(1024, 512)

    mine_q, w_out, kv8 = lax.optimization_barrier((mine_q, w_out, kv8))
    wo = lax.ppermute(
        w_out, ("y", "x"), [(a * 4 + b, b * 4 + a) for a in range(4) for b in range(4)]
    )
    wo4 = jnp.concatenate([wo[:, 256 * j : 256 * j + 256] for j in range(4)], axis=0)
    wq4 = jnp.concatenate([mine_q] + [shift(mine_q, "y", by) for by in SHIFTS[1:]], axis=0)
    wa = jnp.concatenate([wq4, wo4], axis=1)
    wb = shift(wa, "c", 1)
    qd, wq, wo = call(
        qd_kernel, [S, H, H, H],
        [sds((2, 512, 256)), sds((1024, 256)), sds((256, 1024))],
        [pltpu.VMEM((2, 512, 1024), BF), pltpu.VMEM((1024, 256), BF), pltpu.VMEM((256, 1024), BF),
         pltpu.VMEM((512, 256), BF), pltpu.VMEM((512, 256), BF), pltpu.SemaphoreType.DMA((24,))],
        540, 5000, 61, "queries", [H] * 3,
    )(pos, xg, wa, wb)

    pay, att, dq, at, dqt = call(
        attn_kernel, [H, H, V],
        [sds((1024, 512)), sds((512, 256)), sds((512, 256)), sds((256, 512)), sds((256, 512))],
        [pltpu.VMEM((512, 256), BF), pltpu.VMEM((512, 256), BF),
         pltpu.VMEM((256, 1024), BF), pltpu.VMEM((256, 1024), BF),
         pltpu.VMEM((1024, 256), F32), pltpu.VMEM((1024, 256), F32),
         pltpu.VMEM((1024, 512), BF), pltpu.VMEM((4, 16, 1024), BF),
         pltpu.SemaphoreType.DMA((14,))],
        1700, 6000, 56, "attention", [H, V, V, V, V],
    )(xg, qd, kvg)

    red = lax.psum_scatter(pay, "z", scatter_dimension=0, tiled=True)
    md = call(md_kernel, [S] + [V] * 4, [sds((256, 1024))] * 4, [], 540, 4000, 16, "md")(
        pos, att, dq, wq, wo
    )
    md = [md[0]] + [shift(m, "x", by) for m, by in zip(md[1:], SHIFTS[1:])]
    (g,) = call(
        g_kernel, [H, V, V], [sds((8, 128, 512))],
        [pltpu.VMEM((2, 512, 1024), BF), pltpu.VMEM((8, 128, 512), BF), pltpu.SemaphoreType.DMA((8,))],
        540, 4000, 61, "grads", [H],
    )(xg, at, dqt)
    g = lax.all_to_all(g, ("y", "c"), split_axis=0, concat_axis=0, tiled=True)
    gq, go = call(
        gsum_kernel, [V], [sds((128, 256)), sds((32, 1024))], [], 1, 1200, 16, "gsum"
    )(g)
    go = lax.ppermute(
        go, ("y", "x"), [(a * 4 + b, b * 4 + a) for a in range(4) for b in range(4)]
    )
    total = md[0].astype(F32) + md[1].astype(F32) + md[2].astype(F32) + md[3].astype(F32)
    mixed = (tok.astype(F32) + total[0:128]).astype(BF)
    d_tokens = (cot.astype(F32) + total[128:256]).astype(BF)
    red, mixed, d_tokens = lax.optimization_barrier((red, mixed, d_tokens))

    parts = call(
        part_kernel, [S, V, V], [sds((32, 1024))] * 4,
        [pltpu.VMEM((128, 1024), F32)], 134, 2000, 16, "part",
    )(pos, red, wkv)
    gq, *parts = lax.optimization_barrier((gq, *parts))
    (g,) = call(
        split_kernel, [S, V, V], [sds((1280, 128))],
        [pltpu.VMEM((1280, 128), F32), pltpu.VMEM((2, 128, 128), F32), pltpu.VMEM((8, 32, 128), F32)],
        1, 600, 16, "split",
    )(pos, gq, go)
    parts = [parts[0]] + [shift(p, "x", by) for p, by in zip(parts[1:], SHIFTS[1:])]
    g = lax.all_to_all(
        g.reshape(32, 40, 128), ("x", "z"), split_axis=0, concat_axis=0, tiled=True
    ).reshape(1280, 128)
    d_context, g_query, g_out = call(
        finish_kernel, [V] * 5, [sds((32, 1024)), sds((4, 1024), F32), sds((4, 1024), F32)],
        [], 1, 700, 8, "finish",
    )(g, *parts)
    return mixed[None], d_tokens[None], d_context[None], g_query, g_out


def solution(mesh):
    fine = Mesh(mesh.devices.reshape(4, 2, 4, 8), ("y", "c", "x", "z"))
    seq = P(("y", "c"), ("x", "z"), None)
    wts = P(("y", "c"), None)
    grad = P(("y", "c", "x", "z"), None)
    return jax.shard_map(
        local,
        mesh=fine,
        in_specs=(seq, seq, seq, wts, wts, wts, wts, seq),
        out_specs=(seq, seq, seq, grad, grad),
        check_vma=False,
    )
```

```python
import jax
import jax.numpy as jnp
from jax import lax
from jax.experimental import pallas as pl
from jax.experimental.pallas import tpu as pltpu
from jax.sharding import Mesh, PartitionSpec as P

BF = jnp.bfloat16
F32 = jnp.float32
SHIFTS = (0, 1, -1, 2)
Z_SHIFTS = (0, 4, 3, -3, 2, -2, 1, -1)
SIZES = {"y": 4, "c": 2, "x": 4, "z": 8}


def dot(a, b, da, db):
    return lax.dot_general(a, b, (((da,), (db,)), ((), ())), preferred_element_type=F32)


def shift(value, axis, by):
    n = SIZES[axis]
    return lax.ppermute(value, axis, [(i, (i + by) % n) for i in range(n)])


def mod(a, n):
    return lax.rem(a + n, n)


def run_copies(pairs, sems):
    copies = [pltpu.make_async_copy(a, b, sems.at[i]) for i, (a, b) in enumerate(pairs)]
    for copy in copies:
        copy.start()
    return copies


def wait_all(copies):
    for copy in copies:
        copy.wait()


def pack_kernel(tok, cot, pattern, wk, wv, wq, out, cut, pat_s, x_s, w_s, sems):
    cols = pl.ds(pl.multiple_of(256 * lax.axis_index("x"), 256), 256)
    copies = run_copies(
        [
            (pattern, pat_s),
            (wk.at[:, cols], w_s.at[:, pl.ds(0, 256)]),
            (wv.at[:, cols], w_s.at[:, pl.ds(256, 256)]),
            (tok, x_s.at[pl.ds(0, 128), :]),
            (cot, x_s.at[pl.ds(128, 128), :]),
            (wq.at[:, cols], w_s.at[:, pl.ds(512, 256)]),
        ],
        sems,
    )
    block = lax.broadcasted_iota(jnp.int32, (16, 1024), 0)
    key = lax.broadcasted_iota(jnp.int32, (16, 1024), 1)
    grow = jnp.where(block == 4 * ((key // 32) % 4) + key // 256, 1.0, 0.0).astype(BF)
    copies[0].wait()
    rows = jnp.where(pat_s[...] == 1, 1.0, 0.0).astype(BF)
    rows = jnp.concatenate([rows, jnp.zeros((14, 16), BF)], axis=0)
    x_s[256:272, :] = dot(rows, grow, 1, 0).astype(BF)
    wait_all(copies[1:])
    wait_all(run_copies([(w_s, cut), (x_s, out)], sems))


def kv_kernel(c0, c1, c2, c3, wa, wb, kv_out, w_out, wq_out, wo_out, ctx, w_s, wq_s, wo_s, sems):
    y, c, x = lax.axis_index("y"), lax.axis_index("c"), lax.axis_index("x")
    for half, core in ((wa, c), (wb, 1 - c)):
        for slot, by in enumerate(SHIFTS):
            rows = slice(128 * slot, 128 * slot + 128)
            at = pl.multiple_of(128 * (2 * mod(y - by, 4) + core), 128)
            w_s[pl.ds(at, 128), :] = half[rows, 0:512]
            wq_s[pl.ds(at, 128), :] = half[rows, 512:768]
            at = pl.multiple_of(128 * core, 128)
            wo_s[pl.ds(at, 128), 256 * slot : 256 * slot + 256] = half[rows, 768:1024]
    copies = run_copies([(w_s, w_out), (wq_s, wq_out), (wo_s, wo_out)], sems)
    for src, by in zip((c0, c1, c2, c3), SHIFTS):
        at = pl.multiple_of(32 * mod(x - by, 4), 32)
        ctx[pl.ds(at, 32), :] = src[...]
    kv_out[...] = dot(ctx[...], w_s[...], 1, 0).astype(BF)
    wait_all(copies)


def qd_kernel(xg, wq, wo, qd_out, x_s, wq_s, wo_s, qd_s, sems):
    pairs = [(wq, wq_s), (wo, wo_s)]
    for t in range(4):
        for k in range(2):
            rows = pl.ds(128 * t, 128)
            pairs.append((xg.at[t, pl.ds(128 * k, 128), :], x_s.at[k, rows, :]))
    wait_all(run_copies(pairs, sems))
    q = dot(x_s[0], wq_s[...], 1, 0).astype(BF)
    qd_s[0] = q * jnp.asarray(0.125, BF)
    qd_s[1] = dot(x_s[1], wo_s[...], 1, 1).astype(BF)
    wait_all(run_copies([(qd_s, qd_out)], sems))


def attn_kernel(xg, qd, kv0, kv1, kv2, kv3, kv4, kv5, kv6, kv7, pay, att_out, dq_out, kv, q_s, da_s,
                kt_s, vt_s, dk_s, dv_s, at_s, dqt_s, gq_s, go_s, pay_s, mask_s, x_s, sems):
    mask_copies = [
        pltpu.make_async_copy(xg.at[t, pl.ds(256, 16), :], mask_s.at[t], sems.at[t])
        for t in range(4)
    ]
    x_copies = [
        pltpu.make_async_copy(
            xg.at[t, pl.ds(128 * k, 128), :], x_s.at[k, pl.ds(128 * t, 128), :], sems.at[4 + 4 * k + t]
        )
        for t in range(4)
        for k in range(2)
    ]
    mask_copies.append(pltpu.make_async_copy(qd.at[0], q_s, sems.at[20]))
    mask_copies.append(pltpu.make_async_copy(qd.at[1], da_s, sems.at[21]))
    for copy in mask_copies + x_copies:
        copy.start()
    z = lax.axis_index("z")
    for src, by in zip((kv0, kv1, kv2, kv3, kv4, kv5, kv6, kv7), Z_SHIFTS):
        at = pl.multiple_of(128 * mod(z - by, 8), 128)
        kv[pl.ds(at, 128), :] = src[...]
    kt_s[...] = kv[:, 0:256].T
    vt_s[...] = kv[:, 256:512].T
    dk_s[...] = jnp.zeros_like(dk_s)
    dv_s[...] = jnp.zeros_like(dv_s)
    for copy in mask_copies:
        copy.wait()
    lane = lax.broadcasted_iota(jnp.int32, (256, 128), 1) // 64
    row16 = lax.broadcasted_iota(jnp.int32, (16, 128), 0)
    col16 = lax.broadcasted_iota(jnp.int32, (16, 128), 1) // 64
    pick = jnp.where(row16 == col16, 1.0, 0.0).astype(BF)

    allowed = [
        jnp.concatenate([dot(mask_s[2 * u + s], pick, 0, 0) for s in range(2)], axis=1) > 0.5
        for u in range(2)
    ]
    zero = jnp.zeros((256, 128), BF)

    def first(u, h):
        pair = slice(128 * (h // 2), 128 * (h // 2) + 128)
        vpair = slice(256 + 128 * (h // 2), 384 + 128 * (h // 2))
        qrows = slice(256 * u, 256 * u + 256)
        own = lane == (h % 2)
        qm = jnp.where(own, q_s[qrows, pair], zero)
        dam = jnp.where(own, da_s[qrows, pair], zero)
        s = dot(kv[:, pair], qm, 1, 1)
        dp = dot(kv[:, vpair], dam, 1, 1)
        return qm, dam, s, dp

    def second(u, h, qm, dam, s, dp):
        pair = slice(128 * (h // 2), 128 * (h // 2) + 128)
        head = slice(64 * h, 64 * h + 64)
        qrows = slice(256 * u, 256 * u + 256)
        s = jnp.where(allowed[u], s, -jnp.inf)
        e = jnp.exp(s - jnp.max(s, axis=0, keepdims=True))
        p = e * (1.0 / jnp.sum(e, axis=0, keepdims=True))
        plow = p.astype(BF)
        delta = jnp.sum(p * dp, axis=0, keepdims=True)
        ds = (p * (dp - delta)).astype(BF)
        return plow, ds

    def third(u, h, qm, dam, plow, ds):
        pair = slice(128 * (h // 2), 128 * (h // 2) + 128)
        head = slice(64 * h, 64 * h + 64)
        qrows = slice(256 * u, 256 * u + 256)
        at_s[head, qrows] = dot(vt_s[head, :], plow, 1, 0).astype(BF)
        dqt_s[head, qrows] = (0.125 * dot(kt_s[head, :], ds, 1, 0)).astype(BF)
        dv_s[:, pair] += dot(plow, dam, 1, 0)
        dk_s[:, pair] += dot(ds, qm, 1, 0)


    units = [(u, h) for h in range(4) for u in range(2)]

    now = first(*units[0])
    for n, (u, h) in enumerate(units):
        later = first(*units[n + 1]) if n < 7 else None
        plow, ds = second(u, h, *now)
        third(u, h, now[0], now[1], plow, ds)
        now = later
    for copy in x_copies:
        copy.wait()
    go = dot(at_s[...], x_s[1], 1, 0)
    gq = dot(dqt_s[...], x_s[0], 1, 0)
    for j in range(8):
        go_s[j] = go[:, 128 * j : 128 * j + 128]
    for j in range(2):
        gq_s[j] = gq[128 * j : 128 * j + 128, :].T
    outs = []
    for zd in range(8):
        block = slice(128 * zd, 128 * zd + 128)
        pay_s[block, 0:256] = dk_s[block, :].astype(BF)
        pay_s[block, 256:512] = dv_s[block, :].astype(BF)
        for b in range(4):
            rows = slice(128 * zd + 32 * b, 128 * zd + 32 * b + 32)
            for j in range(2):
                lanes = slice(512 + 128 * j, 640 + 128 * j)
                pay_s[rows, lanes] = gq_s[j, pl.ds(4 * zd + b, 32, stride=32), :].astype(BF)
                part = [go_s[2 * b + j, pl.ds(4 * zd + i, 8, stride=32), :] for i in range(4)]
                lanes = slice(768 + 128 * j, 896 + 128 * j)
                pay_s[rows, lanes] = jnp.concatenate(part, axis=0).astype(BF)
        outs.append(pltpu.make_async_copy(pay_s.at[block, :], pay.at[block, :], sems.at[12 + zd]))
        outs[-1].start()
    att_out[...] = at_s[...].T
    dq_out[...] = dqt_s[...].T
    for copy in outs:
        copy.wait()


def md_kernel(att, dq, wq, wo, out):
    for t in range(4):
        rows = slice(128 * t, 128 * t + 128)
        out[t, 0:128, :] = dot(att[rows, :], wo[...], 1, 0).astype(BF)
        out[t, 128:256, :] = dot(dq[rows, :], wq[...], 1, 1).astype(BF)


def split_kernel(red, w, p0, p1, p2, p3, g_out, part, g_s):
    x = lax.axis_index("x")
    part[...] = dot(red[:, 0:256], w[:, 0:256], 1, 1) + dot(red[:, 256:512], w[:, 256:512], 1, 1)
    for out, by in zip((p0, p1, p2, p3), SHIFTS):
        at = pl.multiple_of(32 * mod(x + by, 4), 32)
        out[...] = part[pl.ds(at, 32), :].astype(BF)
    g_s[...] = jnp.zeros_like(g_s)
    for i in range(4):
        for j in range(2):
            lanes = slice(512 + 128 * j, 640 + 128 * j)
            rows = slice(32 * i, 32 * i + 32)
            g_s[pl.ds(2 * i + j, 32, stride=40), :] = red[rows, lanes].astype(F32)
    for b in range(4):
        for j in range(2):
            block = red[32 * b : 32 * b + 32, 768 + 128 * j : 896 + 128 * j].astype(F32)
            for i in range(4):
                at = 320 * x + 8 + 8 * i + 2 * b + j
                g_s[pl.ds(at, 8, stride=40), :] = block[8 * i : 8 * i + 8, :]
    g_out[...] = g_s[...].astype(BF)


def finish_kernel(g, p0, p1, p2, p3, dctx, g_query, g_out):
    total = p0[...].astype(F32)
    for p in (p1, p2, p3):
        total += p[...].astype(F32)
    dctx[...] = total.astype(BF)
    for xs in range(4):
        acc = jnp.zeros((8, 128), F32)
        for yc in range(8):
            at = 40 * (4 * yc + xs)
            acc += g[at : at + 8, :].astype(F32)
        for i in range(4):
            for j in range(2):
                row = 2 * i + j
                lanes = slice(256 * xs + 128 * j, 256 * xs + 128 * j + 128)
                g_query[i : i + 1, lanes] = acc[row : row + 1, :]
    acc = jnp.zeros((32, 128), F32)
    for src in range(32):
        acc += g[40 * src + 8 : 40 * src + 40, :].astype(F32)
    for i in range(4):
        for m in range(8):
            row = 8 * i + m
            g_out[i : i + 1, 128 * m : 128 * m + 128] = acc[row : row + 1, :]


V = pl.BlockSpec(memory_space=pltpu.VMEM)
H = pl.BlockSpec(memory_space=pltpu.HBM)


def sds(shape, dtype=BF):
    return jax.ShapeDtypeStruct(shape, dtype)


def call(kernel, in_specs, outs, scratch, mflop, kib, limit, name, out_specs=None):
    return pl.pallas_call(
        kernel,
        out_shape=outs,
        in_specs=in_specs,
        out_specs=out_specs or [V] * len(outs),
        scratch_shapes=scratch,
        compiler_params=pltpu.CompilerParams(vmem_limit_bytes=limit * 2**20),
        cost_estimate=pl.CostEstimate(
            flops=mflop * 10**6, bytes_accessed=kib * 1024, transcendentals=0
        ),
        name=name,
    )


def local(tokens, context, pattern, w_query, w_key, w_value, w_out, cotangent):
    tok, ctx, cot = tokens[0], context[0], cotangent[0]
    own, mine = call(
        pack_kernel, [H] * 6, [sds((272, 1024)), sds((128, 768))],
        [pltpu.VMEM((2, 16), jnp.int32), pltpu.VMEM((272, 1024), BF), pltpu.VMEM((128, 768), BF),
         pltpu.SemaphoreType.DMA((6,))],
        1, 1500, 61, "pack", [H] * 2,
    )(tok, cot, pattern[0], w_key, w_value, w_query)
    xg = lax.all_gather(own, "x", axis=0, tiled=False)

    wo = lax.ppermute(
        w_out, ("y", "x"), [(a * 4 + b, b * 4 + a) for a in range(4) for b in range(4)]
    )
    wo = jnp.concatenate([wo[:, 256 * j : 256 * j + 256] for j in range(4)], axis=0)
    ctxs = [ctx] + [shift(ctx, "x", by) for by in SHIFTS[1:]]
    wa = jnp.concatenate([mine] + [shift(mine, "y", by) for by in SHIFTS[1:]], axis=0)
    wa = jnp.concatenate([wa, wo], axis=1)
    wa, *ctxs = lax.optimization_barrier((wa, *ctxs))
    wb = shift(wa, "c", 1)
    kv, wkv, wq, wo = call(
        kv_kernel, [V] * 6,
        [sds((128, 512)), sds((1024, 512)), sds((1024, 256)), sds((256, 1024))],
        [pltpu.VMEM((128, 1024), BF), pltpu.VMEM((1024, 512), BF), pltpu.VMEM((1024, 256), BF),
         pltpu.VMEM((256, 1024), BF), pltpu.SemaphoreType.DMA((3,))],
        134, 3000, 16, "kv", [V, H, H, H],
    )(*ctxs, wa, wb)
    kvs = [kv] + [shift(kv, "z", by) for by in Z_SHIFTS[1:]]
    (qd,) = call(
        qd_kernel, [H] * 3, [sds((2, 512, 256))],
        [pltpu.VMEM((2, 512, 1024), BF), pltpu.VMEM((1024, 256), BF), pltpu.VMEM((256, 1024), BF),
         pltpu.VMEM((2, 512, 256), BF), pltpu.SemaphoreType.DMA((10,))],
        540, 5000, 24, "queries", [H],
    )(xg, wq, wo)

    pay, att, dq = call(
        attn_kernel, [H, H] + [V] * 8,
        [sds((1024, 1024)), sds((512, 256)), sds((512, 256))],
        [pltpu.VMEM((1024, 512), BF), pltpu.VMEM((512, 256), BF), pltpu.VMEM((512, 256), BF),
         pltpu.VMEM((256, 1024), BF), pltpu.VMEM((256, 1024), BF),
         pltpu.VMEM((1024, 256), F32), pltpu.VMEM((1024, 256), F32),
         pltpu.VMEM((256, 512), BF), pltpu.VMEM((256, 512), BF),
         pltpu.VMEM((2, 1024, 128), F32), pltpu.VMEM((8, 256, 128), F32),
         pltpu.VMEM((1024, 1024), BF), pltpu.VMEM((4, 16, 1024), BF),
         pltpu.VMEM((2, 512, 1024), BF), pltpu.SemaphoreType.DMA((22,))],
        2200, 8000, 48, "attention", [H, V, V],
    )(xg, qd, *kvs)

    red = lax.psum_scatter(pay, "z", scatter_dimension=0, tiled=True)
    (md,) = call(md_kernel, [V] * 4, [sds((4, 256, 1024))], [], 540, 4000, 16, "md")(
        att, dq, wq, wo
    )
    md = lax.all_to_all(md, "x", split_axis=0, concat_axis=0, tiled=True)
    md = jnp.sum(md.astype(F32), axis=0)
    mixed = (tok.astype(F32) + md[0:128]).astype(BF)
    d_tokens = (cot.astype(F32) + md[128:256]).astype(BF)
    red, mixed, d_tokens = lax.optimization_barrier((red, mixed, d_tokens))

    *parts, g = call(
        split_kernel, [V, V], [sds((32, 1024))] * 4 + [sds((1280, 128))],
        [pltpu.VMEM((128, 1024), F32), pltpu.VMEM((1280, 128), F32)], 134, 2000, 16, "split",
    )(red, wkv)
    parts = [parts[0]] + [shift(p, "x", by) for p, by in zip(parts[1:], SHIFTS[1:])]
    g = lax.all_to_all(
        g.reshape(32, 40, 128), ("y", "c", "x"), split_axis=0, concat_axis=0, tiled=True
    ).reshape(1280, 128)
    d_context, g_query, g_out = call(
        finish_kernel, [V] * 5, [sds((32, 1024)), sds((4, 1024), F32), sds((4, 1024), F32)],
        [], 1, 700, 8, "finish",
    )(g, *parts)
    return mixed[None], d_tokens[None], d_context[None], g_query, g_out


def solution(mesh):
    fine = Mesh(mesh.devices.reshape(4, 2, 4, 8), ("y", "c", "x", "z"))
    seq = P(("y", "c"), ("x", "z"), None)
    wts = P(("y", "c"), None)
    grad = P(("y", "c", "x", "z"), None)
    return jax.shard_map(
        local,
        mesh=fine,
        in_specs=(seq, seq, seq, wts, wts, wts, wts, seq),
        out_specs=(seq, seq, seq, grad, grad),
        check_vma=False,
    )
```

```python
import jax
import jax.numpy as jnp
from jax import lax
from jax.experimental import pallas as pl
from jax.experimental.pallas import tpu as pltpu
from jax.sharding import Mesh, PartitionSpec as P

BF = jnp.bfloat16
F32 = jnp.float32
SHIFTS = (0, 1, -1, 2)
SIZES = {"y": 4, "c": 2, "x": 4, "z": 8}


def dot(a, b, da, db):
    return lax.dot_general(a, b, (((da,), (db,)), ((), ())), preferred_element_type=F32)


def shift(value, axis, by):
    n = SIZES[axis]
    return lax.ppermute(value, axis, [(i, (i + by) % n) for i in range(n)])


def mod(a, n):
    return lax.rem(a + n, n)


def run_copies(pairs, sems):
    copies = [pltpu.make_async_copy(a, b, sems.at[i]) for i, (a, b) in enumerate(pairs)]
    for copy in copies:
        copy.start()
    return copies


def wait_all(copies):
    for copy in copies:
        copy.wait()


def pack_kernel(tok, cot, pattern, wk, wv, wq, out, kv_cut, q_cut, pat_s, x_s, kv_s, q_s, sems):
    cols = pl.ds(pl.multiple_of(256 * lax.axis_index("x"), 256), 256)
    copies = run_copies(
        [
            (pattern, pat_s),
            (wk.at[:, cols], kv_s.at[:, pl.ds(0, 256)]),
            (wv.at[:, cols], kv_s.at[:, pl.ds(256, 256)]),
            (tok, x_s.at[pl.ds(0, 128), :]),
            (cot, x_s.at[pl.ds(128, 128), :]),
            (wq.at[:, cols], q_s),
        ],
        sems,
    )
    block = lax.broadcasted_iota(jnp.int32, (16, 1024), 0)
    key = lax.broadcasted_iota(jnp.int32, (16, 1024), 1)
    grow = jnp.where(block == 4 * ((key // 32) % 4) + key // 256, 1.0, 0.0).astype(BF)
    copies[0].wait()
    rows = jnp.where(pat_s[...] == 1, 1.0, 0.0).astype(BF)
    rows = jnp.concatenate([rows, jnp.zeros((14, 16), BF)], axis=0)
    x_s[256:272, :] = dot(rows, grow, 1, 0).astype(BF)
    wait_all(copies[1:])
    wait_all(run_copies([(x_s, out), (kv_s, kv_cut), (q_s, q_cut)], sems))


def kv_kernel(c0, c1, c2, c3, wa, wb, kv_out, w_out, ctx, w_s, kv_s, sems):
    y, c, x = (lax.axis_index(n) for n in ("y", "c", "x"))
    for half, core in ((wa, c), (wb, 1 - c)):
        for slot, by in enumerate(SHIFTS):
            at = pl.multiple_of(128 * (2 * mod(y - by, 4) + core), 128)
            w_s[pl.ds(at, 128), :] = half[128 * slot : 128 * slot + 128, :]
    for src, by in zip((c0, c1, c2, c3), SHIFTS):
        at = pl.multiple_of(32 * mod(x - by, 4), 32)
        ctx[pl.ds(at, 32), :] = src[...]
    kv_s[...] = dot(ctx[...], w_s[...], 1, 0).astype(BF)
    pairs = [(kv_s, kv_out.at[zd]) for zd in range(8)] + [(w_s, w_out)]
    wait_all(run_copies(pairs, sems))


def qd_kernel(xg, wa, wb, qd_out, wq_out, wo_out, x_s, wq_s, wo_s, q_s, da_s, sems):
    y, c = lax.axis_index("y"), lax.axis_index("c")
    pairs = []
    for half, core in ((wa, c), (wb, 1 - c)):
        for slot, by in enumerate(SHIFTS):
            rows = pl.ds(128 * slot, 128)
            at = pl.multiple_of(128 * (2 * mod(y - by, 4) + core), 128)
            pairs.append((half.at[rows, pl.ds(0, 256)], wq_s.at[pl.ds(at, 128), :]))
            at = pl.multiple_of(128 * core, 128)
            lanes = pl.ds(256 * slot, 256)
            pairs.append((half.at[rows, pl.ds(256, 256)], wo_s.at[pl.ds(at, 128), lanes]))
    for t in range(4):
        for k in range(2):
            rows = pl.ds(128 * t, 128)
            pairs.append((xg.at[t, pl.ds(128 * k, 128), :], x_s.at[k, rows, :]))
    wait_all(run_copies(pairs, sems))
    q = dot(x_s[0], wq_s[...], 1, 0).astype(BF)
    q_s[...] = q * jnp.asarray(0.125, BF)
    da_s[...] = dot(x_s[1], wo_s[...], 1, 1).astype(BF)
    pairs = [(q_s, qd_out.at[0]), (da_s, qd_out.at[1]), (wq_s, wq_out), (wo_s, wo_out)]
    wait_all(run_copies(pairs, sems))


def attn_kernel(xg, qd, kv, pay, att_out, dq_out, q_s, da_s,
                kt_s, vt_s, dk_s, dv_s, at_s, dqt_s, gq_s, go_s, pay_s, mask_s, x_s, sems):
    mask_copies = [
        pltpu.make_async_copy(xg.at[t, pl.ds(256, 16), :], mask_s.at[t], sems.at[t])
        for t in range(4)
    ]
    x_copies = [
        pltpu.make_async_copy(
            xg.at[t, pl.ds(128 * k, 128), :], x_s.at[k, pl.ds(128 * t, 128), :], sems.at[4 + 4 * k + t]
        )
        for t in range(4)
        for k in range(2)
    ]
    mask_copies.append(pltpu.make_async_copy(qd.at[0], q_s, sems.at[20]))
    mask_copies.append(pltpu.make_async_copy(qd.at[1], da_s, sems.at[21]))
    for copy in mask_copies + x_copies:
        copy.start()
    kt_s[...] = kv[:, 0:256].T
    vt_s[...] = kv[:, 256:512].T
    dk_s[...] = jnp.zeros_like(dk_s)
    dv_s[...] = jnp.zeros_like(dv_s)
    for copy in mask_copies:
        copy.wait()
    lane = lax.broadcasted_iota(jnp.int32, (256, 128), 1) // 64
    row16 = lax.broadcasted_iota(jnp.int32, (16, 128), 0)
    col16 = lax.broadcasted_iota(jnp.int32, (16, 128), 1) // 64
    pick = jnp.where(row16 == col16, 1.0, 0.0).astype(BF)

    allowed = [
        jnp.concatenate([dot(mask_s[2 * u + s], pick, 0, 0) for s in range(2)], axis=1) > 0.5
        for u in range(2)
    ]
    zero = jnp.zeros((256, 128), BF)

    def first(u, h):
        pair = slice(128 * (h // 2), 128 * (h // 2) + 128)
        vpair = slice(256 + 128 * (h // 2), 384 + 128 * (h // 2))
        qrows = slice(256 * u, 256 * u + 256)
        own = lane == (h % 2)
        qm = jnp.where(own, q_s[qrows, pair], zero)
        dam = jnp.where(own, da_s[qrows, pair], zero)
        s = dot(kv[:, pair], qm, 1, 1)
        dp = dot(kv[:, vpair], dam, 1, 1)
        return qm, dam, s, dp

    def second(u, h, qm, dam, s, dp):
        pair = slice(128 * (h // 2), 128 * (h // 2) + 128)
        head = slice(64 * h, 64 * h + 64)
        qrows = slice(256 * u, 256 * u + 256)
        s = jnp.where(allowed[u], s, -jnp.inf)
        e = jnp.exp(s - jnp.max(s, axis=0, keepdims=True))
        p = e * (1.0 / jnp.sum(e, axis=0, keepdims=True))
        plow = p.astype(BF)
        delta = jnp.sum(p * dp, axis=0, keepdims=True)
        ds = (p * (dp - delta)).astype(BF)
        return plow, ds

    def third(u, h, qm, dam, plow, ds):
        pair = slice(128 * (h // 2), 128 * (h // 2) + 128)
        head = slice(64 * h, 64 * h + 64)
        qrows = slice(256 * u, 256 * u + 256)
        at_s[head, qrows] = dot(vt_s[head, :], plow, 1, 0).astype(BF)
        dqt_s[head, qrows] = (0.125 * dot(kt_s[head, :], ds, 1, 0)).astype(BF)
        dv_s[:, pair] += dot(plow, dam, 1, 0)
        dk_s[:, pair] += dot(ds, qm, 1, 0)


    units = [(u, h) for h in range(4) for u in range(2)]

    now = first(*units[0])
    for n, (u, h) in enumerate(units):
        later = first(*units[n + 1]) if n < 7 else None
        plow, ds = second(u, h, *now)
        third(u, h, now[0], now[1], plow, ds)
        now = later
    for copy in x_copies:
        copy.wait()
    go = dot(at_s[...], x_s[1], 1, 0)
    gq = dot(dqt_s[...], x_s[0], 1, 0)
    for j in range(8):
        go_s[j] = go[:, 128 * j : 128 * j + 128]
    for j in range(2):
        gq_s[j] = gq[128 * j : 128 * j + 128, :].T
    outs = []
    for zd in range(8):
        block = slice(128 * zd, 128 * zd + 128)
        pay_s[block, 0:256] = dk_s[block, :].astype(BF)
        pay_s[block, 256:512] = dv_s[block, :].astype(BF)
        for b in range(4):
            rows = slice(128 * zd + 32 * b, 128 * zd + 32 * b + 32)
            for j in range(2):
                lanes = slice(512 + 128 * j, 640 + 128 * j)
                pay_s[rows, lanes] = gq_s[j, pl.ds(4 * zd + b, 32, stride=32), :].astype(BF)
                part = [go_s[2 * b + j, pl.ds(4 * zd + i, 8, stride=32), :] for i in range(4)]
                lanes = slice(768 + 128 * j, 896 + 128 * j)
                pay_s[rows, lanes] = jnp.concatenate(part, axis=0).astype(BF)
        outs.append(pltpu.make_async_copy(pay_s.at[block, :], pay.at[block, :], sems.at[12 + zd]))
        outs[-1].start()
    att_out[...] = at_s[...].T
    dq_out[...] = dqt_s[...].T
    for copy in outs:
        copy.wait()


def md_kernel(att, dq, wq, wo, out):
    for t in range(4):
        rows = slice(128 * t, 128 * t + 128)
        out[t, 0:128, :] = dot(att[rows, :], wo[...], 1, 0).astype(BF)
        out[t, 128:256, :] = dot(dq[rows, :], wq[...], 1, 1).astype(BF)


def split_kernel(red, w, p0, p1, p2, p3, g_out, part, g_s):
    x = lax.axis_index("x")
    part[...] = dot(red[:, 0:256], w[:, 0:256], 1, 1) + dot(red[:, 256:512], w[:, 256:512], 1, 1)
    for out, by in zip((p0, p1, p2, p3), SHIFTS):
        at = pl.multiple_of(32 * mod(x + by, 4), 32)
        out[...] = part[pl.ds(at, 32), :].astype(BF)
    g_s[...] = jnp.zeros_like(g_s)
    for i in range(4):
        for j in range(2):
            lanes = slice(512 + 128 * j, 640 + 128 * j)
            rows = slice(32 * i, 32 * i + 32)
            g_s[pl.ds(2 * i + j, 32, stride=40), :] = red[rows, lanes].astype(F32)
    for b in range(4):
        for j in range(2):
            block = red[32 * b : 32 * b + 32, 768 + 128 * j : 896 + 128 * j].astype(F32)
            for i in range(4):
                at = 320 * x + 8 + 8 * i + 2 * b + j
                g_s[pl.ds(at, 8, stride=40), :] = block[8 * i : 8 * i + 8, :]
    g_out[...] = g_s[...].astype(BF)


def finish_kernel(g, p0, p1, p2, p3, dctx, g_query, g_out):
    total = p0[...].astype(F32)
    for p in (p1, p2, p3):
        total += p[...].astype(F32)
    dctx[...] = total.astype(BF)
    for xs in range(4):
        acc = jnp.zeros((8, 128), F32)
        for yc in range(8):
            at = 40 * (4 * yc + xs)
            acc += g[at : at + 8, :].astype(F32)
        for i in range(4):
            for j in range(2):
                row = 2 * i + j
                lanes = slice(256 * xs + 128 * j, 256 * xs + 128 * j + 128)
                g_query[i : i + 1, lanes] = acc[row : row + 1, :]
    acc = jnp.zeros((32, 128), F32)
    for src in range(32):
        acc += g[40 * src + 8 : 40 * src + 40, :].astype(F32)
    for i in range(4):
        for m in range(8):
            row = 8 * i + m
            g_out[i : i + 1, 128 * m : 128 * m + 128] = acc[row : row + 1, :]


V = pl.BlockSpec(memory_space=pltpu.VMEM)
H = pl.BlockSpec(memory_space=pltpu.HBM)


def sds(shape, dtype=BF):
    return jax.ShapeDtypeStruct(shape, dtype)


def call(kernel, in_specs, outs, scratch, mflop, kib, limit, name, out_specs=None):
    return pl.pallas_call(
        kernel,
        out_shape=outs,
        in_specs=in_specs,
        out_specs=out_specs or [V] * len(outs),
        scratch_shapes=scratch,
        compiler_params=pltpu.CompilerParams(vmem_limit_bytes=limit * 2**20),
        cost_estimate=pl.CostEstimate(
            flops=mflop * 10**6, bytes_accessed=kib * 1024, transcendentals=0
        ),
        name=name,
    )


def local(tokens, context, pattern, w_query, w_key, w_value, w_out, cotangent):
    tok, ctx, cot = tokens[0], context[0], cotangent[0]
    own, mine, mine_q = call(
        pack_kernel, [H] * 6, [sds((272, 1024)), sds((128, 512)), sds((128, 256))],
        [pltpu.VMEM((2, 16), jnp.int32), pltpu.VMEM((272, 1024), BF), pltpu.VMEM((128, 512), BF),
         pltpu.VMEM((128, 256), BF), pltpu.SemaphoreType.DMA((6,))],
        1, 1500, 61, "pack", [H] * 3,
    )(tok, cot, pattern[0], w_key, w_value, w_query)
    xg = lax.all_gather(own, "x", axis=0, tiled=False)

    ctxs = [ctx] + [shift(ctx, "x", by) for by in SHIFTS[1:]]
    wa = jnp.concatenate([mine] + [shift(mine, "y", by) for by in SHIFTS[1:]], axis=0)
    wa, *ctxs = lax.optimization_barrier((wa, *ctxs))
    wb = shift(wa, "c", 1)
    kv8, wkv = call(
        kv_kernel, [V] * 6, [sds((8, 128, 512)), sds((1024, 512))],
        [pltpu.VMEM((128, 1024), BF), pltpu.VMEM((1024, 512), BF), pltpu.VMEM((128, 512), BF),
         pltpu.SemaphoreType.DMA((9,))],
        134, 3000, 16, "kv", [H, H],
    )(*ctxs, wa, wb)
    kvg = lax.all_to_all(kv8, "z", split_axis=0, concat_axis=0, tiled=True).reshape(1024, 512)

    mine_q, w_out, kv8 = lax.optimization_barrier((mine_q, w_out, kv8))
    wo = lax.ppermute(
        w_out, ("y", "x"), [(a * 4 + b, b * 4 + a) for a in range(4) for b in range(4)]
    )
    wo4 = jnp.concatenate([wo[:, 256 * j : 256 * j + 256] for j in range(4)], axis=0)
    wq4 = jnp.concatenate([mine_q] + [shift(mine_q, "y", by) for by in SHIFTS[1:]], axis=0)
    wa = jnp.concatenate([wq4, wo4], axis=1)
    wb = shift(wa, "c", 1)
    qd, wq, wo = call(
        qd_kernel, [H, H, H],
        [sds((2, 512, 256)), sds((1024, 256)), sds((256, 1024))],
        [pltpu.VMEM((2, 512, 1024), BF), pltpu.VMEM((1024, 256), BF), pltpu.VMEM((256, 1024), BF),
         pltpu.VMEM((512, 256), BF), pltpu.VMEM((512, 256), BF), pltpu.SemaphoreType.DMA((24,))],
        540, 5000, 61, "queries", [H] * 3,
    )(xg, wa, wb)

    pay, att, dq = call(
        attn_kernel, [H, H, V],
        [sds((1024, 1024)), sds((512, 256)), sds((512, 256))],
        [pltpu.VMEM((512, 256), BF), pltpu.VMEM((512, 256), BF),
         pltpu.VMEM((256, 1024), BF), pltpu.VMEM((256, 1024), BF),
         pltpu.VMEM((1024, 256), F32), pltpu.VMEM((1024, 256), F32),
         pltpu.VMEM((256, 512), BF), pltpu.VMEM((256, 512), BF),
         pltpu.VMEM((2, 1024, 128), F32), pltpu.VMEM((8, 256, 128), F32),
         pltpu.VMEM((1024, 1024), BF), pltpu.VMEM((4, 16, 1024), BF),
         pltpu.VMEM((2, 512, 1024), BF), pltpu.SemaphoreType.DMA((22,))],
        2200, 8000, 48, "attention", [H, V, V],
    )(xg, qd, kvg)

    red = lax.psum_scatter(pay, "z", scatter_dimension=0, tiled=True)
    (md,) = call(md_kernel, [V] * 4, [sds((4, 256, 1024))], [], 540, 4000, 16, "md")(
        att, dq, wq, wo
    )
    md = lax.all_to_all(md, "x", split_axis=0, concat_axis=0, tiled=True)
    md = jnp.sum(md.astype(F32), axis=0)
    mixed = (tok.astype(F32) + md[0:128]).astype(BF)
    d_tokens = (cot.astype(F32) + md[128:256]).astype(BF)
    red, mixed, d_tokens = lax.optimization_barrier((red, mixed, d_tokens))

    *parts, g = call(
        split_kernel, [V, V], [sds((32, 1024))] * 4 + [sds((1280, 128))],
        [pltpu.VMEM((128, 1024), F32), pltpu.VMEM((1280, 128), F32)], 134, 2000, 16, "split",
    )(red, wkv)
    parts = [parts[0]] + [shift(p, "x", by) for p, by in zip(parts[1:], SHIFTS[1:])]
    g = lax.all_to_all(
        g.reshape(32, 40, 128), ("y", "c", "x"), split_axis=0, concat_axis=0, tiled=True
    ).reshape(1280, 128)
    d_context, g_query, g_out = call(
        finish_kernel, [V] * 5, [sds((32, 1024)), sds((4, 1024), F32), sds((4, 1024), F32)],
        [], 1, 700, 8, "finish",
    )(g, *parts)
    return mixed[None], d_tokens[None], d_context[None], g_query, g_out


def solution(mesh):
    fine = Mesh(mesh.devices.reshape(4, 2, 4, 8), ("y", "c", "x", "z"))
    seq = P(("y", "c"), ("x", "z"), None)
    wts = P(("y", "c"), None)
    grad = P(("y", "c", "x", "z"), None)
    return jax.shard_map(
        local,
        mesh=fine,
        in_specs=(seq, seq, seq, wts, wts, wts, wts, seq),
        out_specs=(seq, seq, seq, grad, grad),
        check_vma=False,
    )
```

```python
import jax
import jax.numpy as jnp
from jax import lax
from jax.experimental import pallas as pl
from jax.experimental.pallas import tpu as pltpu
from jax.sharding import Mesh, PartitionSpec as P

BF = jnp.bfloat16
F32 = jnp.float32
SHIFTS = (0, 1, -1, 2)
SIZES = {"y": 4, "c": 2, "x": 4, "z": 8}


def dot(a, b, da, db):
    return lax.dot_general(a, b, (((da,), (db,)), ((), ())), preferred_element_type=F32)


def shift(value, axis, by):
    n = SIZES[axis]
    return lax.ppermute(value, axis, [(i, (i + by) % n) for i in range(n)])


def mod(a, n):
    return lax.rem(a + n, n)


def run_copies(pairs, sems):
    copies = [pltpu.make_async_copy(a, b, sems.at[i]) for i, (a, b) in enumerate(pairs)]
    for copy in copies:
        copy.start()
    return copies


def wait_all(copies):
    for copy in copies:
        copy.wait()


def pack_kernel(tok, cot, pattern, wk, wv, wq, out, kv_cut, q_cut, pat_s, x_s, kv_s, q_s, sems):
    cols = pl.ds(pl.multiple_of(256 * lax.axis_index("x"), 256), 256)
    copies = run_copies(
        [
            (pattern, pat_s),
            (wk.at[:, cols], kv_s.at[:, pl.ds(0, 256)]),
            (wv.at[:, cols], kv_s.at[:, pl.ds(256, 256)]),
            (tok, x_s.at[pl.ds(0, 128), :]),
            (cot, x_s.at[pl.ds(128, 128), :]),
            (wq.at[:, cols], q_s),
        ],
        sems,
    )
    block = lax.broadcasted_iota(jnp.int32, (16, 1024), 0)
    key = lax.broadcasted_iota(jnp.int32, (16, 1024), 1)
    grow = jnp.where(block == 4 * ((key // 32) % 4) + key // 256, 1.0, 0.0).astype(BF)
    copies[0].wait()
    rows = jnp.where(pat_s[...] == 1, 1.0, 0.0).astype(BF)
    rows = jnp.concatenate([rows, jnp.zeros((14, 16), BF)], axis=0)
    x_s[256:272, :] = dot(rows, grow, 1, 0).astype(BF)
    wait_all(copies[1:])
    wait_all(run_copies([(x_s, out), (kv_s, kv_cut), (q_s, q_cut)], sems))


def kv_kernel(c0, c1, c2, c3, wa, wb, kv_out, w_out, ctx, w_s, kv_s, sems):
    y, c, x = (lax.axis_index(n) for n in ("y", "c", "x"))
    for half, core in ((wa, c), (wb, 1 - c)):
        for slot, by in enumerate(SHIFTS):
            at = pl.multiple_of(128 * (2 * mod(y - by, 4) + core), 128)
            w_s[pl.ds(at, 128), :] = half[128 * slot : 128 * slot + 128, :]
    for src, by in zip((c0, c1, c2, c3), SHIFTS):
        at = pl.multiple_of(32 * mod(x - by, 4), 32)
        ctx[pl.ds(at, 32), :] = src[...]
    kv_s[...] = dot(ctx[...], w_s[...], 1, 0).astype(BF)
    pairs = [(kv_s, kv_out.at[zd]) for zd in range(8)] + [(w_s, w_out)]
    wait_all(run_copies(pairs, sems))


def qd_kernel(xg, wa, wb, qd_out, wq_out, wo_out, x_s, wq_s, wo_s, q_s, da_s, sems):
    y, c = lax.axis_index("y"), lax.axis_index("c")
    pairs = []
    for half, core in ((wa, c), (wb, 1 - c)):
        for slot, by in enumerate(SHIFTS):
            rows = pl.ds(128 * slot, 128)
            at = pl.multiple_of(128 * (2 * mod(y - by, 4) + core), 128)
            pairs.append((half.at[rows, pl.ds(0, 256)], wq_s.at[pl.ds(at, 128), :]))
            at = pl.multiple_of(128 * core, 128)
            lanes = pl.ds(256 * slot, 256)
            pairs.append((half.at[rows, pl.ds(256, 256)], wo_s.at[pl.ds(at, 128), lanes]))
    for t in range(4):
        for k in range(2):
            rows = pl.ds(128 * t, 128)
            pairs.append((xg.at[t, pl.ds(128 * k, 128), :], x_s.at[k, rows, :]))
    wait_all(run_copies(pairs, sems))
    q = dot(x_s[0], wq_s[...], 1, 0).astype(BF)
    q_s[...] = q * jnp.asarray(0.125, BF)
    da_s[...] = dot(x_s[1], wo_s[...], 1, 1).astype(BF)
    pairs = [(q_s, qd_out.at[0]), (da_s, qd_out.at[1]), (wq_s, wq_out), (wo_s, wo_out)]
    wait_all(run_copies(pairs, sems))


def attn_kernel(xg, qd, kv, pay, att_out, dq_out, q_s, da_s,
                kt_s, vt_s, dk_s, dv_s, at_s, dqt_s, gq_s, go_s, pay_s, mask_s, x_s, sems):
    mask_copies = [
        pltpu.make_async_copy(xg.at[t, pl.ds(256, 16), :], mask_s.at[t], sems.at[t])
        for t in range(4)
    ]
    x_copies = [
        pltpu.make_async_copy(
            xg.at[t, pl.ds(128 * k, 128), :], x_s.at[k, pl.ds(128 * t, 128), :], sems.at[4 + 4 * k + t]
        )
        for t in range(4)
        for k in range(2)
    ]
    mask_copies.append(pltpu.make_async_copy(qd.at[0], q_s, sems.at[20]))
    mask_copies.append(pltpu.make_async_copy(qd.at[1], da_s, sems.at[21]))
    for copy in mask_copies + x_copies:
        copy.start()
    kt_s[...] = kv[:, 0:256].T
    vt_s[...] = kv[:, 256:512].T
    dk_s[...] = jnp.zeros_like(dk_s)
    dv_s[...] = jnp.zeros_like(dv_s)
    for copy in mask_copies:
        copy.wait()
    lane = lax.broadcasted_iota(jnp.int32, (256, 128), 1) // 64
    row16 = lax.broadcasted_iota(jnp.int32, (16, 128), 0)
    col16 = lax.broadcasted_iota(jnp.int32, (16, 128), 1) // 64
    pick = jnp.where(row16 == col16, 1.0, 0.0).astype(BF)

    allowed = [
        jnp.concatenate([dot(mask_s[2 * u + s], pick, 0, 0) for s in range(2)], axis=1) > 0.5
        for u in range(2)
    ]
    zero = jnp.zeros((256, 128), BF)

    def first(u, h):
        pair = slice(128 * (h // 2), 128 * (h // 2) + 128)
        vpair = slice(256 + 128 * (h // 2), 384 + 128 * (h // 2))
        qrows = slice(256 * u, 256 * u + 256)
        own = lane == (h % 2)
        qm = jnp.where(own, q_s[qrows, pair], zero)
        dam = jnp.where(own, da_s[qrows, pair], zero)
        s = dot(kv[:, pair], qm, 1, 1)
        dp = dot(kv[:, vpair], dam, 1, 1)
        return qm, dam, s, dp

    def second(u, h, qm, dam, s, dp):
        pair = slice(128 * (h // 2), 128 * (h // 2) + 128)
        head = slice(64 * h, 64 * h + 64)
        qrows = slice(256 * u, 256 * u + 256)
        s = jnp.where(allowed[u], s, -jnp.inf)
        e = jnp.exp(s - jnp.max(s, axis=0, keepdims=True))
        p = e * (1.0 / jnp.sum(e, axis=0, keepdims=True))
        plow = p.astype(BF)
        delta = jnp.sum(p * dp, axis=0, keepdims=True)
        ds = (p * (dp - delta)).astype(BF)
        return plow, ds

    def third(u, h, qm, dam, plow, ds):
        pair = slice(128 * (h // 2), 128 * (h // 2) + 128)
        head = slice(64 * h, 64 * h + 64)
        qrows = slice(256 * u, 256 * u + 256)
        at_s[head, qrows] = dot(vt_s[head, :], plow, 1, 0).astype(BF)
        dqt_s[head, qrows] = (0.125 * dot(kt_s[head, :], ds, 1, 0)).astype(BF)
        dv_s[:, pair] += dot(plow, dam, 1, 0)
        dk_s[:, pair] += dot(ds, qm, 1, 0)


    units = [(u, h) for h in range(4) for u in range(2)]

    now = first(*units[0])
    for n, (u, h) in enumerate(units):
        later = first(*units[n + 1]) if n < 7 else None
        plow, ds = second(u, h, *now)
        third(u, h, now[0], now[1], plow, ds)
        now = later
    for copy in x_copies:
        copy.wait()
    go = dot(at_s[...], x_s[1], 1, 0)
    gq = dot(dqt_s[...], x_s[0], 1, 0)
    for j in range(8):
        go_s[j] = go[:, 128 * j : 128 * j + 128]
    for j in range(2):
        gq_s[j] = gq[128 * j : 128 * j + 128, :].T
    outs = []
    for zd in range(8):
        block = slice(128 * zd, 128 * zd + 128)
        pay_s[block, 0:256] = dk_s[block, :].astype(BF)
        pay_s[block, 256:512] = dv_s[block, :].astype(BF)
        for b in range(4):
            rows = slice(128 * zd + 32 * b, 128 * zd + 32 * b + 32)
            for j in range(2):
                lanes = slice(512 + 128 * j, 640 + 128 * j)
                pay_s[rows, lanes] = gq_s[j, pl.ds(4 * zd + b, 32, stride=32), :].astype(BF)
                part = [go_s[2 * b + j, pl.ds(4 * zd + i, 8, stride=32), :] for i in range(4)]
                lanes = slice(768 + 128 * j, 896 + 128 * j)
                pay_s[rows, lanes] = jnp.concatenate(part, axis=0).astype(BF)
        outs.append(pltpu.make_async_copy(pay_s.at[block, :], pay.at[block, :], sems.at[12 + zd]))
        outs[-1].start()
    att_out[...] = at_s[...].T
    dq_out[...] = dqt_s[...].T
    for copy in outs:
        copy.wait()


def md_kernel(att, dq, wq, wo, out):
    for t in range(4):
        rows = slice(128 * t, 128 * t + 128)
        out[t, 0:128, :] = dot(att[rows, :], wo[...], 1, 0).astype(BF)
        out[t, 128:256, :] = dot(dq[rows, :], wq[...], 1, 1).astype(BF)


def part_kernel(red, w, part):
    total = dot(red[:, 0:256], w[:, 0:256], 1, 1) + dot(red[:, 256:512], w[:, 256:512], 1, 1)
    part[...] = total.astype(BF)


def split_kernel(red, g_out, g_s):
    x = lax.axis_index("x")
    g_s[...] = jnp.zeros_like(g_s)
    for i in range(4):
        for j in range(2):
            lanes = slice(512 + 128 * j, 640 + 128 * j)
            rows = slice(32 * i, 32 * i + 32)
            g_s[pl.ds(2 * i + j, 32, stride=40), :] = red[rows, lanes].astype(F32)
    for b in range(4):
        for j in range(2):
            block = red[32 * b : 32 * b + 32, 768 + 128 * j : 896 + 128 * j].astype(F32)
            for i in range(4):
                at = 320 * x + 8 + 8 * i + 2 * b + j
                g_s[pl.ds(at, 8, stride=40), :] = block[8 * i : 8 * i + 8, :]
    g_out[...] = g_s[...].astype(BF)


def finish_kernel(g, g_query, g_out):
    for xs in range(4):
        acc = jnp.zeros((8, 128), F32)
        for yc in range(8):
            at = 40 * (4 * yc + xs)
            acc += g[at : at + 8, :].astype(F32)
        for i in range(4):
            for j in range(2):
                row = 2 * i + j
                lanes = slice(256 * xs + 128 * j, 256 * xs + 128 * j + 128)
                g_query[i : i + 1, lanes] = acc[row : row + 1, :]
    acc = jnp.zeros((32, 128), F32)
    for src in range(32):
        acc += g[40 * src + 8 : 40 * src + 40, :].astype(F32)
    for i in range(4):
        for m in range(8):
            row = 8 * i + m
            g_out[i : i + 1, 128 * m : 128 * m + 128] = acc[row : row + 1, :]


V = pl.BlockSpec(memory_space=pltpu.VMEM)
H = pl.BlockSpec(memory_space=pltpu.HBM)


def sds(shape, dtype=BF):
    return jax.ShapeDtypeStruct(shape, dtype)


def call(kernel, in_specs, outs, scratch, mflop, kib, limit, name, out_specs=None):
    return pl.pallas_call(
        kernel,
        out_shape=outs,
        in_specs=in_specs,
        out_specs=out_specs or [V] * len(outs),
        scratch_shapes=scratch,
        compiler_params=pltpu.CompilerParams(vmem_limit_bytes=limit * 2**20),
        cost_estimate=pl.CostEstimate(
            flops=mflop * 10**6, bytes_accessed=kib * 1024, transcendentals=0
        ),
        name=name,
    )


def local(tokens, context, pattern, w_query, w_key, w_value, w_out, cotangent):
    tok, ctx, cot = tokens[0], context[0], cotangent[0]
    own, mine, mine_q = call(
        pack_kernel, [H] * 6, [sds((272, 1024)), sds((128, 512)), sds((128, 256))],
        [pltpu.VMEM((2, 16), jnp.int32), pltpu.VMEM((272, 1024), BF), pltpu.VMEM((128, 512), BF),
         pltpu.VMEM((128, 256), BF), pltpu.SemaphoreType.DMA((6,))],
        1, 1500, 61, "pack", [H] * 3,
    )(tok, cot, pattern[0], w_key, w_value, w_query)
    xg = lax.all_gather(own, "x", axis=0, tiled=False)

    ctxs = [ctx] + [shift(ctx, "x", by) for by in SHIFTS[1:]]
    wa = jnp.concatenate([mine] + [shift(mine, "y", by) for by in SHIFTS[1:]], axis=0)
    wa, *ctxs = lax.optimization_barrier((wa, *ctxs))
    wb = shift(wa, "c", 1)
    kv8, wkv = call(
        kv_kernel, [V] * 6, [sds((8, 128, 512)), sds((1024, 512))],
        [pltpu.VMEM((128, 1024), BF), pltpu.VMEM((1024, 512), BF), pltpu.VMEM((128, 512), BF),
         pltpu.SemaphoreType.DMA((9,))],
        134, 3000, 16, "kv", [H, H],
    )(*ctxs, wa, wb)
    kvg = lax.all_to_all(kv8, "z", split_axis=0, concat_axis=0, tiled=True).reshape(1024, 512)

    mine_q, w_out, kv8 = lax.optimization_barrier((mine_q, w_out, kv8))
    wo = lax.ppermute(
        w_out, ("y", "x"), [(a * 4 + b, b * 4 + a) for a in range(4) for b in range(4)]
    )
    wo4 = jnp.concatenate([wo[:, 256 * j : 256 * j + 256] for j in range(4)], axis=0)
    wq4 = jnp.concatenate([mine_q] + [shift(mine_q, "y", by) for by in SHIFTS[1:]], axis=0)
    wa = jnp.concatenate([wq4, wo4], axis=1)
    wb = shift(wa, "c", 1)
    qd, wq, wo = call(
        qd_kernel, [H, H, H],
        [sds((2, 512, 256)), sds((1024, 256)), sds((256, 1024))],
        [pltpu.VMEM((2, 512, 1024), BF), pltpu.VMEM((1024, 256), BF), pltpu.VMEM((256, 1024), BF),
         pltpu.VMEM((512, 256), BF), pltpu.VMEM((512, 256), BF), pltpu.SemaphoreType.DMA((24,))],
        540, 5000, 61, "queries", [H] * 3,
    )(xg, wa, wb)

    pay, att, dq = call(
        attn_kernel, [H, H, V],
        [sds((1024, 1024)), sds((512, 256)), sds((512, 256))],
        [pltpu.VMEM((512, 256), BF), pltpu.VMEM((512, 256), BF),
         pltpu.VMEM((256, 1024), BF), pltpu.VMEM((256, 1024), BF),
         pltpu.VMEM((1024, 256), F32), pltpu.VMEM((1024, 256), F32),
         pltpu.VMEM((256, 512), BF), pltpu.VMEM((256, 512), BF),
         pltpu.VMEM((2, 1024, 128), F32), pltpu.VMEM((8, 256, 128), F32),
         pltpu.VMEM((1024, 1024), BF), pltpu.VMEM((4, 16, 1024), BF),
         pltpu.VMEM((2, 512, 1024), BF), pltpu.SemaphoreType.DMA((22,))],
        2200, 8000, 48, "attention", [H, V, V],
    )(xg, qd, kvg)

    red = lax.psum_scatter(pay, "z", scatter_dimension=0, tiled=True)
    (md,) = call(md_kernel, [V] * 4, [sds((4, 256, 1024))], [], 540, 4000, 16, "md")(
        att, dq, wq, wo
    )
    md = lax.all_to_all(md, "x", split_axis=0, concat_axis=0, tiled=True)
    md = jnp.sum(md.astype(F32), axis=0)
    mixed = (tok.astype(F32) + md[0:128]).astype(BF)
    d_tokens = (cot.astype(F32) + md[128:256]).astype(BF)
    red, mixed, d_tokens = lax.optimization_barrier((red, mixed, d_tokens))

    (part,) = call(part_kernel, [V, V], [sds((128, 1024))], [], 134, 2000, 16, "part")(red, wkv)
    d_context = lax.psum_scatter(part, "x", scatter_dimension=0, tiled=True)
    (g,) = call(
        split_kernel, [V], [sds((1280, 128))], [pltpu.VMEM((1280, 128), F32)], 1, 600, 16, "split"
    )(red)
    g = lax.all_to_all(
        g.reshape(32, 40, 128), ("y", "c", "x"), split_axis=0, concat_axis=0, tiled=True
    ).reshape(1280, 128)
    g_query, g_out = call(
        finish_kernel, [V], [sds((4, 1024), F32), sds((4, 1024), F32)], [], 1, 700, 8, "finish"
    )(g)
    return mixed[None], d_tokens[None], d_context[None], g_query, g_out


def solution(mesh):
    fine = Mesh(mesh.devices.reshape(4, 2, 4, 8), ("y", "c", "x", "z"))
    seq = P(("y", "c"), ("x", "z"), None)
    wts = P(("y", "c"), None)
    grad = P(("y", "c", "x", "z"), None)
    return jax.shard_map(
        local,
        mesh=fine,
        in_specs=(seq, seq, seq, wts, wts, wts, wts, seq),
        out_specs=(seq, seq, seq, grad, grad),
        check_vma=False,
    )
```

```python
import jax
import jax.numpy as jnp
from jax import lax
from jax.experimental import pallas as pl
from jax.experimental.pallas import tpu as pltpu
from jax.sharding import Mesh, PartitionSpec as P

BF = jnp.bfloat16
F32 = jnp.float32
SHIFTS = (0, 1, -1, 2)
SIZES = {"y": 4, "c": 2, "x": 4, "z": 8}


def dot(a, b, da, db):
    return lax.dot_general(a, b, (((da,), (db,)), ((), ())), preferred_element_type=F32)


def shift(value, axis, by):
    n = SIZES[axis]
    return lax.ppermute(value, axis, [(i, (i + by) % n) for i in range(n)])


def mod(a, n):
    return lax.rem(a + n, n)


def run_copies(pairs, sems):
    copies = [pltpu.make_async_copy(a, b, sems.at[i]) for i, (a, b) in enumerate(pairs)]
    for copy in copies:
        copy.start()
    return copies


def wait_all(copies):
    for copy in copies:
        copy.wait()


def pack_kernel(tok, cot, pattern, wk, wv, wq, out, kv_cut, q_cut, pat_s, x_s, kv_s, q_s, sems):
    cols = pl.ds(pl.multiple_of(256 * lax.axis_index("x"), 256), 256)
    copies = run_copies(
        [
            (pattern, pat_s),
            (wk.at[:, cols], kv_s.at[:, pl.ds(0, 256)]),
            (wv.at[:, cols], kv_s.at[:, pl.ds(256, 256)]),
            (tok, x_s.at[pl.ds(0, 128), :]),
            (cot, x_s.at[pl.ds(128, 128), :]),
            (wq.at[:, cols], q_s),
        ],
        sems,
    )
    block = lax.broadcasted_iota(jnp.int32, (16, 1024), 0)
    key = lax.broadcasted_iota(jnp.int32, (16, 1024), 1)
    grow = jnp.where(block == 4 * ((key // 32) % 4) + key // 256, 1.0, 0.0).astype(BF)
    copies[0].wait()
    rows = jnp.where(pat_s[...] == 1, 1.0, 0.0).astype(BF)
    rows = jnp.concatenate([rows, jnp.zeros((14, 16), BF)], axis=0)
    x_s[256:272, :] = dot(rows, grow, 1, 0).astype(BF)
    wait_all(copies[1:])
    wait_all(run_copies([(x_s, out), (kv_s, kv_cut), (q_s, q_cut)], sems))


def kv_kernel(c0, c1, c2, c3, wa, wb, kv_out, w_out, ctx, w_s, kv_s, sems):
    y, c, x = (lax.axis_index(n) for n in ("y", "c", "x"))
    for half, core in ((wa, c), (wb, 1 - c)):
        for slot, by in enumerate(SHIFTS):
            at = pl.multiple_of(128 * (2 * mod(y - by, 4) + core), 128)
            w_s[pl.ds(at, 128), :] = half[128 * slot : 128 * slot + 128, :]
    for src, by in zip((c0, c1, c2, c3), SHIFTS):
        at = pl.multiple_of(32 * mod(x - by, 4), 32)
        ctx[pl.ds(at, 32), :] = src[...]
    kv_s[...] = dot(ctx[...], w_s[...], 1, 0).astype(BF)
    pairs = [(kv_s, kv_out.at[zd]) for zd in range(8)] + [(w_s, w_out)]
    wait_all(run_copies(pairs, sems))


def qd_kernel(xg, wa, wb, qd_out, wq_out, wo_out, x_s, wq_s, wo_s, q_s, da_s, sems):
    y, c = lax.axis_index("y"), lax.axis_index("c")
    pairs = []
    for half, core in ((wa, c), (wb, 1 - c)):
        for slot, by in enumerate(SHIFTS):
            rows = pl.ds(128 * slot, 128)
            at = pl.multiple_of(128 * (2 * mod(y - by, 4) + core), 128)
            pairs.append((half.at[rows, pl.ds(0, 256)], wq_s.at[pl.ds(at, 128), :]))
            at = pl.multiple_of(128 * core, 128)
            lanes = pl.ds(256 * slot, 256)
            pairs.append((half.at[rows, pl.ds(256, 256)], wo_s.at[pl.ds(at, 128), lanes]))
    for t in range(4):
        for k in range(2):
            rows = pl.ds(128 * t, 128)
            pairs.append((xg.at[t, pl.ds(128 * k, 128), :], x_s.at[k, rows, :]))
    wait_all(run_copies(pairs, sems))
    q = dot(x_s[0], wq_s[...], 1, 0).astype(BF)
    q_s[...] = q * jnp.asarray(0.125, BF)
    da_s[...] = dot(x_s[1], wo_s[...], 1, 1).astype(BF)
    pairs = [(q_s, qd_out.at[0]), (da_s, qd_out.at[1]), (wq_s, wq_out), (wo_s, wo_out)]
    wait_all(run_copies(pairs, sems))


def attn_kernel(xg, qd, kv, pay, at_s, dqt_s, q_s, da_s,
                kt_s, vt_s, dk_s, dv_s, gq_s, go_s, pay_s, mask_s, x_s, sems):
    mask_copies = [
        pltpu.make_async_copy(xg.at[t, pl.ds(256, 16), :], mask_s.at[t], sems.at[t])
        for t in range(4)
    ]
    x_copies = [
        pltpu.make_async_copy(
            xg.at[t, pl.ds(128 * k, 128), :], x_s.at[k, pl.ds(128 * t, 128), :], sems.at[4 + 4 * k + t]
        )
        for t in range(4)
        for k in range(2)
    ]
    mask_copies.append(pltpu.make_async_copy(qd.at[0], q_s, sems.at[20]))
    mask_copies.append(pltpu.make_async_copy(qd.at[1], da_s, sems.at[21]))
    for copy in mask_copies + x_copies:
        copy.start()
    kt_s[...] = kv[:, 0:256].T
    vt_s[...] = kv[:, 256:512].T
    dk_s[...] = jnp.zeros_like(dk_s)
    dv_s[...] = jnp.zeros_like(dv_s)
    for copy in mask_copies:
        copy.wait()
    lane = lax.broadcasted_iota(jnp.int32, (256, 128), 1) // 64
    row16 = lax.broadcasted_iota(jnp.int32, (16, 128), 0)
    col16 = lax.broadcasted_iota(jnp.int32, (16, 128), 1) // 64
    pick = jnp.where(row16 == col16, 1.0, 0.0).astype(BF)

    allowed = [
        jnp.concatenate([dot(mask_s[2 * u + s], pick, 0, 0) for s in range(2)], axis=1) > 0.5
        for u in range(2)
    ]
    zero = jnp.zeros((256, 128), BF)

    def first(u, h):
        pair = slice(128 * (h // 2), 128 * (h // 2) + 128)
        vpair = slice(256 + 128 * (h // 2), 384 + 128 * (h // 2))
        qrows = slice(256 * u, 256 * u + 256)
        own = lane == (h % 2)
        qm = jnp.where(own, q_s[qrows, pair], zero)
        dam = jnp.where(own, da_s[qrows, pair], zero)
        s = dot(kv[:, pair], qm, 1, 1)
        dp = dot(kv[:, vpair], dam, 1, 1)
        return qm, dam, s, dp

    def second(u, h, qm, dam, s, dp):
        pair = slice(128 * (h // 2), 128 * (h // 2) + 128)
        head = slice(64 * h, 64 * h + 64)
        qrows = slice(256 * u, 256 * u + 256)
        s = jnp.where(allowed[u], s, -jnp.inf)
        e = jnp.exp(s - jnp.max(s, axis=0, keepdims=True))
        p = e * (1.0 / jnp.sum(e, axis=0, keepdims=True))
        plow = p.astype(BF)
        delta = jnp.sum(p * dp, axis=0, keepdims=True)
        ds = (p * (dp - delta)).astype(BF)
        return plow, ds

    def third(u, h, qm, dam, plow, ds):
        pair = slice(128 * (h // 2), 128 * (h // 2) + 128)
        head = slice(64 * h, 64 * h + 64)
        qrows = slice(256 * u, 256 * u + 256)
        at_s[head, qrows] = dot(vt_s[head, :], plow, 1, 0).astype(BF)
        dqt_s[head, qrows] = (0.125 * dot(kt_s[head, :], ds, 1, 0)).astype(BF)
        dv_s[:, pair] += dot(plow, dam, 1, 0)
        dk_s[:, pair] += dot(ds, qm, 1, 0)


    units = [(u, h) for h in range(4) for u in range(2)]

    now = first(*units[0])
    for n, (u, h) in enumerate(units):
        later = first(*units[n + 1]) if n < 7 else None
        plow, ds = second(u, h, *now)
        third(u, h, now[0], now[1], plow, ds)
        now = later
    for copy in x_copies:
        copy.wait()
    go = dot(at_s[...], x_s[1], 1, 0)
    gq = dot(dqt_s[...], x_s[0], 1, 0)
    for j in range(8):
        go_s[j] = go[:, 128 * j : 128 * j + 128]
    for j in range(2):
        gq_s[j] = gq[128 * j : 128 * j + 128, :].T
    outs = []
    for zd in range(8):
        block = slice(128 * zd, 128 * zd + 128)
        pay_s[block, 0:256] = dk_s[block, :].astype(BF)
        pay_s[block, 256:512] = dv_s[block, :].astype(BF)
        for b in range(4):
            rows = slice(128 * zd + 32 * b, 128 * zd + 32 * b + 32)
            for j in range(2):
                lanes = slice(512 + 128 * j, 640 + 128 * j)
                pay_s[rows, lanes] = gq_s[j, pl.ds(4 * zd + b, 32, stride=32), :].astype(BF)
                part = [go_s[2 * b + j, pl.ds(4 * zd + i, 8, stride=32), :] for i in range(4)]
                lanes = slice(768 + 128 * j, 896 + 128 * j)
                pay_s[rows, lanes] = jnp.concatenate(part, axis=0).astype(BF)
        outs.append(pltpu.make_async_copy(pay_s.at[block, :], pay.at[block, :], sems.at[12 + zd]))
        outs[-1].start()
    for copy in outs:
        copy.wait()


def md_kernel(att, dq, wq, wo, out):
    for t in range(4):
        rows = slice(128 * t, 128 * t + 128)
        out[t, 0:128, :] = dot(att[:, rows], wo[...], 0, 0).astype(BF)
        out[t, 128:256, :] = dot(dq[:, rows], wq[...], 0, 1).astype(BF)


def split_kernel(red, w, p0, p1, p2, p3, g_out, part, g_s):
    x = lax.axis_index("x")
    part[...] = dot(red[:, 0:256], w[:, 0:256], 1, 1) + dot(red[:, 256:512], w[:, 256:512], 1, 1)
    for out, by in zip((p0, p1, p2, p3), SHIFTS):
        at = pl.multiple_of(32 * mod(x + by, 4), 32)
        out[...] = part[pl.ds(at, 32), :].astype(BF)
    g_s[...] = jnp.zeros_like(g_s)
    for i in range(4):
        for j in range(2):
            lanes = slice(512 + 128 * j, 640 + 128 * j)
            rows = slice(32 * i, 32 * i + 32)
            g_s[pl.ds(2 * i + j, 32, stride=40), :] = red[rows, lanes].astype(F32)
    for b in range(4):
        for j in range(2):
            block = red[32 * b : 32 * b + 32, 768 + 128 * j : 896 + 128 * j].astype(F32)
            for i in range(4):
                at = 320 * x + 8 + 8 * i + 2 * b + j
                g_s[pl.ds(at, 8, stride=40), :] = block[8 * i : 8 * i + 8, :]
    g_out[...] = g_s[...].astype(BF)


def finish_kernel(g, p0, p1, p2, p3, dctx, g_query, g_out):
    total = p0[...].astype(F32)
    for p in (p1, p2, p3):
        total += p[...].astype(F32)
    dctx[...] = total.astype(BF)
    for xs in range(4):
        acc = jnp.zeros((8, 128), F32)
        for yc in range(8):
            at = 40 * (4 * yc + xs)
            acc += g[at : at + 8, :].astype(F32)
        for i in range(4):
            for j in range(2):
                row = 2 * i + j
                lanes = slice(256 * xs + 128 * j, 256 * xs + 128 * j + 128)
                g_query[i : i + 1, lanes] = acc[row : row + 1, :]
    acc = jnp.zeros((32, 128), F32)
    for src in range(32):
        acc += g[40 * src + 8 : 40 * src + 40, :].astype(F32)
    for i in range(4):
        for m in range(8):
            row = 8 * i + m
            g_out[i : i + 1, 128 * m : 128 * m + 128] = acc[row : row + 1, :]


V = pl.BlockSpec(memory_space=pltpu.VMEM)
H = pl.BlockSpec(memory_space=pltpu.HBM)


def sds(shape, dtype=BF):
    return jax.ShapeDtypeStruct(shape, dtype)


def call(kernel, in_specs, outs, scratch, mflop, kib, limit, name, out_specs=None):
    return pl.pallas_call(
        kernel,
        out_shape=outs,
        in_specs=in_specs,
        out_specs=out_specs or [V] * len(outs),
        scratch_shapes=scratch,
        compiler_params=pltpu.CompilerParams(vmem_limit_bytes=limit * 2**20),
        cost_estimate=pl.CostEstimate(
            flops=mflop * 10**6, bytes_accessed=kib * 1024, transcendentals=0
        ),
        name=name,
    )


def local(tokens, context, pattern, w_query, w_key, w_value, w_out, cotangent):
    tok, ctx, cot = tokens[0], context[0], cotangent[0]
    own, mine, mine_q = call(
        pack_kernel, [H] * 6, [sds((272, 1024)), sds((128, 512)), sds((128, 256))],
        [pltpu.VMEM((2, 16), jnp.int32), pltpu.VMEM((272, 1024), BF), pltpu.VMEM((128, 512), BF),
         pltpu.VMEM((128, 256), BF), pltpu.SemaphoreType.DMA((6,))],
        1, 1500, 61, "pack", [H] * 3,
    )(tok, cot, pattern[0], w_key, w_value, w_query)
    xg = lax.all_gather(own, "x", axis=0, tiled=False)

    ctxs = [ctx] + [shift(ctx, "x", by) for by in SHIFTS[1:]]
    wa = jnp.concatenate([mine] + [shift(mine, "y", by) for by in SHIFTS[1:]], axis=0)
    wa, *ctxs = lax.optimization_barrier((wa, *ctxs))
    wb = shift(wa, "c", 1)
    kv8, wkv = call(
        kv_kernel, [V] * 6, [sds((8, 128, 512)), sds((1024, 512))],
        [pltpu.VMEM((128, 1024), BF), pltpu.VMEM((1024, 512), BF), pltpu.VMEM((128, 512), BF),
         pltpu.SemaphoreType.DMA((9,))],
        134, 3000, 16, "kv", [H, H],
    )(*ctxs, wa, wb)
    kvg = lax.all_to_all(kv8, "z", split_axis=0, concat_axis=0, tiled=True).reshape(1024, 512)

    mine_q, w_out, kv8 = lax.optimization_barrier((mine_q, w_out, kv8))
    wo = lax.ppermute(
        w_out, ("y", "x"), [(a * 4 + b, b * 4 + a) for a in range(4) for b in range(4)]
    )
    wo4 = jnp.concatenate([wo[:, 256 * j : 256 * j + 256] for j in range(4)], axis=0)
    wq4 = jnp.concatenate([mine_q] + [shift(mine_q, "y", by) for by in SHIFTS[1:]], axis=0)
    wa = jnp.concatenate([wq4, wo4], axis=1)
    wb = shift(wa, "c", 1)
    qd, wq, wo = call(
        qd_kernel, [H, H, H],
        [sds((2, 512, 256)), sds((1024, 256)), sds((256, 1024))],
        [pltpu.VMEM((2, 512, 1024), BF), pltpu.VMEM((1024, 256), BF), pltpu.VMEM((256, 1024), BF),
         pltpu.VMEM((512, 256), BF), pltpu.VMEM((512, 256), BF), pltpu.SemaphoreType.DMA((24,))],
        540, 5000, 61, "queries", [H] * 3,
    )(xg, wa, wb)

    pay, att, dq = call(
        attn_kernel, [H, H, V],
        [sds((1024, 1024)), sds((256, 512)), sds((256, 512))],
        [pltpu.VMEM((512, 256), BF), pltpu.VMEM((512, 256), BF),
         pltpu.VMEM((256, 1024), BF), pltpu.VMEM((256, 1024), BF),
         pltpu.VMEM((1024, 256), F32), pltpu.VMEM((1024, 256), F32),
         pltpu.VMEM((2, 1024, 128), F32), pltpu.VMEM((8, 256, 128), F32),
         pltpu.VMEM((1024, 1024), BF), pltpu.VMEM((4, 16, 1024), BF),
         pltpu.VMEM((2, 512, 1024), BF), pltpu.SemaphoreType.DMA((22,))],
        2200, 8000, 48, "attention", [H, V, V],
    )(xg, qd, kvg)

    red = lax.psum_scatter(pay, "z", scatter_dimension=0, tiled=True)
    (md,) = call(md_kernel, [V] * 4, [sds((4, 256, 1024))], [], 540, 4000, 16, "md")(
        att, dq, wq, wo
    )
    md = lax.all_to_all(md, "x", split_axis=0, concat_axis=0, tiled=True)
    md = jnp.sum(md.astype(F32), axis=0)
    mixed = (tok.astype(F32) + md[0:128]).astype(BF)
    d_tokens = (cot.astype(F32) + md[128:256]).astype(BF)
    red, mixed, d_tokens = lax.optimization_barrier((red, mixed, d_tokens))

    *parts, g = call(
        split_kernel, [V, V], [sds((32, 1024))] * 4 + [sds((1280, 128))],
        [pltpu.VMEM((128, 1024), F32), pltpu.VMEM((1280, 128), F32)], 134, 2000, 16, "split",
    )(red, wkv)
    parts = [parts[0]] + [shift(p, "x", by) for p, by in zip(parts[1:], SHIFTS[1:])]
    g = lax.all_to_all(
        g.reshape(32, 40, 128), ("y", "c", "x"), split_axis=0, concat_axis=0, tiled=True
    ).reshape(1280, 128)
    d_context, g_query, g_out = call(
        finish_kernel, [V] * 5, [sds((32, 1024)), sds((4, 1024), F32), sds((4, 1024), F32)],
        [], 1, 700, 8, "finish",
    )(g, *parts)
    return mixed[None], d_tokens[None], d_context[None], g_query, g_out


def solution(mesh):
    fine = Mesh(mesh.devices.reshape(4, 2, 4, 8), ("y", "c", "x", "z"))
    seq = P(("y", "c"), ("x", "z"), None)
    wts = P(("y", "c"), None)
    grad = P(("y", "c", "x", "z"), None)
    return jax.shard_map(
        local,
        mesh=fine,
        in_specs=(seq, seq, seq, wts, wts, wts, wts, seq),
        out_specs=(seq, seq, seq, grad, grad),
        check_vma=False,
    )
```

```python
import jax
import jax.numpy as jnp
from jax import lax
from jax.experimental import pallas as pl
from jax.experimental.pallas import tpu as pltpu
from jax.sharding import Mesh, PartitionSpec as P

BF = jnp.bfloat16
F32 = jnp.float32
SHIFTS = (0, 1, -1, 2)
SIZES = {"y": 4, "c": 2, "x": 4, "z": 8}


def dot(a, b, da, db):
    return lax.dot_general(a, b, (((da,), (db,)), ((), ())), preferred_element_type=F32)


def shift(value, axis, by):
    n = SIZES[axis]
    return lax.ppermute(value, axis, [(i, (i + by) % n) for i in range(n)])


def mod(a, n):
    return lax.rem(a + n, n)


def run_copies(pairs, sems):
    copies = [pltpu.make_async_copy(a, b, sems.at[i]) for i, (a, b) in enumerate(pairs)]
    for copy in copies:
        copy.start()
    return copies


def wait_all(copies):
    for copy in copies:
        copy.wait()


def pack_kernel(tok, cot, pattern, wk, wv, wq, out, kv_cut, q_cut, pat_s, x_s, kv_s, q_s, sems):
    cols = pl.ds(pl.multiple_of(256 * lax.axis_index("x"), 256), 256)
    copies = run_copies(
        [
            (pattern, pat_s),
            (wk.at[:, cols], kv_s.at[:, pl.ds(0, 256)]),
            (wv.at[:, cols], kv_s.at[:, pl.ds(256, 256)]),
            (tok, x_s.at[pl.ds(0, 128), :]),
            (cot, x_s.at[pl.ds(128, 128), :]),
            (wq.at[:, cols], q_s),
        ],
        sems,
    )
    block = lax.broadcasted_iota(jnp.int32, (16, 1024), 0)
    key = lax.broadcasted_iota(jnp.int32, (16, 1024), 1)
    grow = jnp.where(block == 4 * ((key // 32) % 4) + key // 256, 1.0, 0.0).astype(BF)
    copies[0].wait()
    rows = jnp.where(pat_s[...] == 1, 1.0, 0.0).astype(BF)
    rows = jnp.concatenate([rows, jnp.zeros((14, 16), BF)], axis=0)
    x_s[256:272, :] = dot(rows, grow, 1, 0).astype(BF)
    wait_all(copies[1:])
    wait_all(run_copies([(x_s, out), (kv_s, kv_cut), (q_s, q_cut)], sems))


def kv_kernel(c0, c1, c2, c3, wa, wb, kv_out, w_out, ctx, w_s, kv_s, sems):
    y, c, x = (lax.axis_index(n) for n in ("y", "c", "x"))
    for half, core in ((wa, c), (wb, 1 - c)):
        for slot, by in enumerate(SHIFTS):
            at = pl.multiple_of(128 * (2 * mod(y - by, 4) + core), 128)
            w_s[pl.ds(at, 128), :] = half[128 * slot : 128 * slot + 128, :]
    for src, by in zip((c0, c1, c2, c3), SHIFTS):
        at = pl.multiple_of(32 * mod(x - by, 4), 32)
        ctx[pl.ds(at, 32), :] = src[...]
    kv_s[...] = dot(ctx[...], w_s[...], 1, 0).astype(BF)
    pairs = [(kv_s, kv_out.at[zd]) for zd in range(8)] + [(w_s, w_out)]
    wait_all(run_copies(pairs, sems))


def qd_kernel(xg, wa, wb, qd_out, wq_out, wo_out, x_s, wq_s, wo_s, q_s, da_s, sems):
    y, c = lax.axis_index("y"), lax.axis_index("c")
    pairs = []
    for half, core in ((wa, c), (wb, 1 - c)):
        for slot, by in enumerate(SHIFTS):
            rows = pl.ds(128 * slot, 128)
            at = pl.multiple_of(128 * (2 * mod(y - by, 4) + core), 128)
            pairs.append((half.at[rows, pl.ds(0, 256)], wq_s.at[pl.ds(at, 128), :]))
            at = pl.multiple_of(128 * core, 128)
            lanes = pl.ds(256 * slot, 256)
            pairs.append((half.at[rows, pl.ds(256, 256)], wo_s.at[pl.ds(at, 128), lanes]))
    for t in range(4):
        for k in range(2):
            rows = pl.ds(128 * t, 128)
            pairs.append((xg.at[t, pl.ds(128 * k, 128), :], x_s.at[k, rows, :]))
    wait_all(run_copies(pairs, sems))
    q = dot(x_s[0], wq_s[...], 1, 0).astype(BF)
    q_s[...] = q * jnp.asarray(0.125, BF)
    da_s[...] = dot(x_s[1], wo_s[...], 1, 1).astype(BF)
    pairs = [(q_s, qd_out.at[0]), (da_s, qd_out.at[1]), (wq_s, wq_out), (wo_s, wo_out)]
    wait_all(run_copies(pairs, sems))


def attn_kernel(xg, qd, kv, pay, at_s, dqt_s, q_s, da_s,
                kt_s, vt_s, dk_s, dv_s, gq_s, go_s, pay_s, mask_s, x_s, sems):
    mask_copies = [
        pltpu.make_async_copy(xg.at[t, pl.ds(256, 16), :], mask_s.at[t], sems.at[t])
        for t in range(4)
    ]
    x_copies = [
        pltpu.make_async_copy(
            xg.at[t, pl.ds(128 * k, 128), :], x_s.at[k, pl.ds(128 * t, 128), :], sems.at[4 + 4 * k + t]
        )
        for t in range(4)
        for k in range(2)
    ]
    mask_copies.append(pltpu.make_async_copy(qd.at[0], q_s, sems.at[20]))
    mask_copies.append(pltpu.make_async_copy(qd.at[1], da_s, sems.at[21]))
    for copy in mask_copies + x_copies:
        copy.start()
    kt_s[...] = kv[:, 0:256].T
    vt_s[...] = kv[:, 256:512].T
    dk_s[...] = jnp.zeros_like(dk_s)
    dv_s[...] = jnp.zeros_like(dv_s)
    for copy in mask_copies:
        copy.wait()
    lane = lax.broadcasted_iota(jnp.int32, (256, 128), 1) // 64
    row16 = lax.broadcasted_iota(jnp.int32, (16, 128), 0)
    col16 = lax.broadcasted_iota(jnp.int32, (16, 128), 1) // 64
    pick = jnp.where(row16 == col16, 1.0, 0.0).astype(BF)

    allowed = [
        jnp.concatenate([dot(mask_s[2 * u + s], pick, 0, 0) for s in range(2)], axis=1) > 0.5
        for u in range(2)
    ]
    zero = jnp.zeros((256, 128), BF)

    def first(u, h):
        pair = slice(128 * (h // 2), 128 * (h // 2) + 128)
        vpair = slice(256 + 128 * (h // 2), 384 + 128 * (h // 2))
        qrows = slice(256 * u, 256 * u + 256)
        own = lane == (h % 2)
        qm = jnp.where(own, q_s[qrows, pair], zero)
        dam = jnp.where(own, da_s[qrows, pair], zero)
        s = dot(kv[:, pair], qm, 1, 1)
        dp = dot(kv[:, vpair], dam, 1, 1)
        return qm, dam, s, dp

    def second(u, h, qm, dam, s, dp):
        pair = slice(128 * (h // 2), 128 * (h // 2) + 128)
        head = slice(64 * h, 64 * h + 64)
        qrows = slice(256 * u, 256 * u + 256)
        s = jnp.where(allowed[u], s, -jnp.inf)
        e = jnp.exp(s - jnp.max(s, axis=0, keepdims=True))
        p = e * (1.0 / jnp.sum(e, axis=0, keepdims=True))
        plow = p.astype(BF)
        delta = jnp.sum(p * dp, axis=0, keepdims=True)
        ds = (p * (dp - delta)).astype(BF)
        return plow, ds

    def third(u, h, qm, dam, plow, ds):
        pair = slice(128 * (h // 2), 128 * (h // 2) + 128)
        head = slice(64 * h, 64 * h + 64)
        qrows = slice(256 * u, 256 * u + 256)
        at_s[head, qrows] = dot(vt_s[head, :], plow, 1, 0).astype(BF)
        dqt_s[head, qrows] = (0.125 * dot(kt_s[head, :], ds, 1, 0)).astype(BF)
        dv_s[:, pair] += dot(plow, dam, 1, 0)
        dk_s[:, pair] += dot(ds, qm, 1, 0)


    units = [(u, h) for h in range(4) for u in range(2)]

    now = first(*units[0])
    for n, (u, h) in enumerate(units):
        later = first(*units[n + 1]) if n < 7 else None
        plow, ds = second(u, h, *now)
        third(u, h, now[0], now[1], plow, ds)
        now = later
    for copy in x_copies:
        copy.wait()
    go = dot(at_s[...], x_s[1], 1, 0)
    gq = dot(dqt_s[...], x_s[0], 1, 0)
    for j in range(8):
        go_s[j] = go[:, 128 * j : 128 * j + 128]
    for j in range(2):
        gq_s[j] = gq[128 * j : 128 * j + 128, :].T
    outs = []
    for zd in range(8):
        block = slice(128 * zd, 128 * zd + 128)
        pay_s[block, 0:256] = dk_s[block, :].astype(BF)
        pay_s[block, 256:512] = dv_s[block, :].astype(BF)
        for b in range(4):
            rows = slice(128 * zd + 32 * b, 128 * zd + 32 * b + 32)
            for j in range(2):
                lanes = slice(512 + 128 * j, 640 + 128 * j)
                pay_s[rows, lanes] = gq_s[j, pl.ds(4 * zd + b, 32, stride=32), :].astype(BF)
                part = [go_s[2 * b + j, pl.ds(4 * zd + i, 8, stride=32), :] for i in range(4)]
                lanes = slice(768 + 128 * j, 896 + 128 * j)
                pay_s[rows, lanes] = jnp.concatenate(part, axis=0).astype(BF)
        outs.append(pltpu.make_async_copy(pay_s.at[block, :], pay.at[block, :], sems.at[12 + zd]))
        outs[-1].start()
    for copy in outs:
        copy.wait()


def md_kernel(att, dq, wq, wo, out):
    for t in range(4):
        rows = slice(128 * t, 128 * t + 128)
        out[t, 0:128, :] = dot(att[:, rows], wo[...], 0, 0).astype(BF)
        out[t, 128:256, :] = dot(dq[:, rows], wq[...], 0, 1).astype(BF)


def split_kernel(red, w, p0, p1, p2, p3, g_out, part, g_s):
    x = lax.axis_index("x")
    part[...] = dot(red[:, 0:256], w[:, 0:256], 1, 1) + dot(red[:, 256:512], w[:, 256:512], 1, 1)
    for out, by in zip((p0, p1, p2, p3), SHIFTS):
        at = pl.multiple_of(32 * mod(x + by, 4), 32)
        out[...] = part[pl.ds(at, 32), :].astype(BF)
    g_s[...] = jnp.zeros_like(g_s)
    for i in range(4):
        for j in range(2):
            lanes = slice(512 + 128 * j, 640 + 128 * j)
            rows = slice(32 * i, 32 * i + 32)
            g_s[pl.ds(2 * i + j, 32, stride=40), :] = red[rows, lanes].astype(F32)
    for b in range(4):
        for j in range(2):
            block = red[32 * b : 32 * b + 32, 768 + 128 * j : 896 + 128 * j].astype(F32)
            for i in range(4):
                at = 320 * x + 8 + 8 * i + 2 * b + j
                g_s[pl.ds(at, 8, stride=40), :] = block[8 * i : 8 * i + 8, :]
    g_out[...] = g_s[...].astype(BF)


def finish_kernel(g, p0, p1, p2, p3, dctx, g_query, g_out):
    total = p0[...].astype(F32)
    for p in (p1, p2, p3):
        total += p[...].astype(F32)
    dctx[...] = total.astype(BF)
    for xs in range(4):
        acc = jnp.zeros((8, 128), F32)
        for yc in range(8):
            at = 40 * (4 * yc + xs)
            acc += g[at : at + 8, :].astype(F32)
        for i in range(4):
            for j in range(2):
                row = 2 * i + j
                lanes = slice(256 * xs + 128 * j, 256 * xs + 128 * j + 128)
                g_query[i : i + 1, lanes] = acc[row : row + 1, :]
    acc = jnp.zeros((32, 128), F32)
    for src in range(32):
        acc += g[40 * src + 8 : 40 * src + 40, :].astype(F32)
    for i in range(4):
        for m in range(8):
            row = 8 * i + m
            g_out[i : i + 1, 128 * m : 128 * m + 128] = acc[row : row + 1, :]


V = pl.BlockSpec(memory_space=pltpu.VMEM)
H = pl.BlockSpec(memory_space=pltpu.HBM)


def sds(shape, dtype=BF):
    return jax.ShapeDtypeStruct(shape, dtype)


def call(kernel, in_specs, outs, scratch, mflop, kib, limit, name, out_specs=None):
    return pl.pallas_call(
        kernel,
        out_shape=outs,
        in_specs=in_specs,
        out_specs=out_specs or [V] * len(outs),
        scratch_shapes=scratch,
        compiler_params=pltpu.CompilerParams(vmem_limit_bytes=limit * 2**20),
        cost_estimate=pl.CostEstimate(
            flops=mflop * 10**6, bytes_accessed=kib * 1024, transcendentals=0
        ),
        name=name,
    )


def local(tokens, context, pattern, w_query, w_key, w_value, w_out, cotangent):
    tok, ctx, cot = tokens[0], context[0], cotangent[0]
    own, mine, mine_q = call(
        pack_kernel, [H] * 6, [sds((272, 1024)), sds((128, 512)), sds((128, 256))],
        [pltpu.VMEM((2, 16), jnp.int32), pltpu.VMEM((272, 1024), BF), pltpu.VMEM((128, 512), BF),
         pltpu.VMEM((128, 256), BF), pltpu.SemaphoreType.DMA((6,))],
        1, 1500, 61, "pack", [H] * 3,
    )(tok, cot, pattern[0], w_key, w_value, w_query)
    xg = lax.all_gather(own, "x", axis=0, tiled=False)

    ctxs = [ctx] + [shift(ctx, "x", by) for by in SHIFTS[1:]]
    wa = jnp.concatenate([mine] + [shift(mine, "y", by) for by in SHIFTS[1:]], axis=0)
    wa, *ctxs = lax.optimization_barrier((wa, *ctxs))
    wb = shift(wa, "c", 1)
    kv8, wkv = call(
        kv_kernel, [V] * 6, [sds((8, 128, 512)), sds((1024, 512))],
        [pltpu.VMEM((128, 1024), BF), pltpu.VMEM((1024, 512), BF), pltpu.VMEM((128, 512), BF),
         pltpu.SemaphoreType.DMA((9,))],
        134, 3000, 16, "kv", [H, H],
    )(*ctxs, wa, wb)
    kvg = lax.all_to_all(kv8, "z", split_axis=0, concat_axis=0, tiled=True).reshape(1024, 512)

    mine_q, w_out, kv8 = lax.optimization_barrier((mine_q, w_out, kv8))
    wo = lax.ppermute(
        w_out, ("y", "x"), [(a * 4 + b, b * 4 + a) for a in range(4) for b in range(4)]
    )
    wo4 = jnp.concatenate([wo[:, 256 * j : 256 * j + 256] for j in range(4)], axis=0)
    wq4 = jnp.concatenate([mine_q] + [shift(mine_q, "y", by) for by in SHIFTS[1:]], axis=0)
    wa = jnp.concatenate([wq4, wo4], axis=1)
    wb = shift(wa, "c", 1)
    qd, wq, wo = call(
        qd_kernel, [H, H, H],
        [sds((2, 512, 256)), sds((1024, 256)), sds((256, 1024))],
        [pltpu.VMEM((2, 512, 1024), BF), pltpu.VMEM((1024, 256), BF), pltpu.VMEM((256, 1024), BF),
         pltpu.VMEM((512, 256), BF), pltpu.VMEM((512, 256), BF), pltpu.SemaphoreType.DMA((24,))],
        540, 5000, 24, "queries", [H] * 3,
    )(xg, wa, wb)

    pay, att, dq = call(
        attn_kernel, [H, H, V],
        [sds((1024, 1024)), sds((256, 512)), sds((256, 512))],
        [pltpu.VMEM((512, 256), BF), pltpu.VMEM((512, 256), BF),
         pltpu.VMEM((256, 1024), BF), pltpu.VMEM((256, 1024), BF),
         pltpu.VMEM((1024, 256), F32), pltpu.VMEM((1024, 256), F32),
         pltpu.VMEM((2, 1024, 128), F32), pltpu.VMEM((8, 256, 128), F32),
         pltpu.VMEM((1024, 1024), BF), pltpu.VMEM((4, 16, 1024), BF),
         pltpu.VMEM((2, 512, 1024), BF), pltpu.SemaphoreType.DMA((22,))],
        2200, 8000, 48, "attention", [H, V, V],
    )(xg, qd, kvg)

    red = lax.psum_scatter(pay, "z", scatter_dimension=0, tiled=True)
    (md,) = call(md_kernel, [V] * 4, [sds((4, 256, 1024))], [], 540, 4000, 16, "md")(
        att, dq, wq, wo
    )
    md = lax.all_to_all(md, "x", split_axis=0, concat_axis=0, tiled=True)
    md = jnp.sum(md.astype(F32), axis=0)
    mixed = (tok.astype(F32) + md[0:128]).astype(BF)
    d_tokens = (cot.astype(F32) + md[128:256]).astype(BF)
    red, mixed, d_tokens = lax.optimization_barrier((red, mixed, d_tokens))

    *parts, g = call(
        split_kernel, [V, V], [sds((32, 1024))] * 4 + [sds((1280, 128))],
        [pltpu.VMEM((128, 1024), F32), pltpu.VMEM((1280, 128), F32)], 134, 2000, 16, "split",
    )(red, wkv)
    parts = [parts[0]] + [shift(p, "x", by) for p, by in zip(parts[1:], SHIFTS[1:])]
    g = lax.all_to_all(
        g.reshape(32, 40, 128), ("y", "c", "x"), split_axis=0, concat_axis=0, tiled=True
    ).reshape(1280, 128)
    d_context, g_query, g_out = call(
        finish_kernel, [V] * 5, [sds((32, 1024)), sds((4, 1024), F32), sds((4, 1024), F32)],
        [], 1, 700, 8, "finish",
    )(g, *parts)
    return mixed[None], d_tokens[None], d_context[None], g_query, g_out


def solution(mesh):
    fine = Mesh(mesh.devices.reshape(4, 2, 4, 8), ("y", "c", "x", "z"))
    seq = P(("y", "c"), ("x", "z"), None)
    wts = P(("y", "c"), None)
    grad = P(("y", "c", "x", "z"), None)
    return jax.shard_map(
        local,
        mesh=fine,
        in_specs=(seq, seq, seq, wts, wts, wts, wts, seq),
        out_specs=(seq, seq, seq, grad, grad),
        check_vma=False,
    )
```
